512 devices in a mesh: wide: 32 (over z_hi, y, core), narrow: 16 (over x, z_lo).
Axes of the slice: x: 4, y: 8, z: 8 (z_hi: 2, z_lo: 4; z = z_hi * 4 + z_lo), core: 2. Of those that a mesh axis runs over, the one named last changes fastest.
Arguments:
- image_embed: bfloat16 [8192, 1152], P(('wide', 'narrow')), may hold values from -0.59765625 to 0.59765625
- text_embed: bfloat16 [8192, 1152], P(('wide', 'narrow')), may hold values from -0.59765625 to 0.59765625
- logit_scale: float32 [1], replicated, may hold values from 2 to 8
- logit_bias: float32 [1], replicated, may hold values from -8 to -4
Outputs:
- loss: float32 [1], replicated
- image_grad: float32 [8192, 1152], P(('wide', 'narrow'))
- text_grad: float32 [8192, 1152], P(('wide', 'narrow'))
The draws below stay inside these ranges and needn't reach their ends.
All inputs are finite; a program needn't handle non-finite values.
Results may differ from the reference program's by a relative error of at most 0.0025.
Values may be sent and summed in bfloat16 or wider, within the bound.
A program may use at most 64 MiB of HBM per device.

```python
import math
import jax
import jax.numpy as jnp
from jax import lax

D = 1152
PAIRS = 8192


def level_of(key, shape, split, low, largest):
    gain, own = 1.0, jax.random.fold_in(key, 6)
    for position, parts in split:
        draws = jnp.exp(jax.random.uniform(jax.random.fold_in(own, position), (parts,), jnp.float32, low / len(split), largest / len(split)))
        gain = gain * jnp.repeat(draws, shape[position] // parts).reshape([-1 if axis == position else 1 for axis in range(len(shape))])
    return gain


def normal_values(stream_key, dims, width, limit, split=(), kind=jnp.bfloat16):
    gain = level_of(stream_key, dims, split, -0.22, 0.18) if split else 1.0
    array = jax.random.normal(stream_key, dims, jnp.float32) * width * gain
    return jnp.minimum(jnp.maximum(array, -limit), limit).astype(kind)


def setup_inputs(seed: int = 0) -> dict:
    key_of = jax.random.split(jax.random.key(seed), 5)
    return {
        "image_embed": normal_values(key_of[0], (PAIRS, D), 0.1, 0.59765625, ((0, 512),)),
        "text_embed": normal_values(key_of[1], (PAIRS, D), 0.1, 0.59765625, ((0, 512),)),
        "logit_scale": jnp.clip(jnp.exp(jax.random.uniform(key_of[2], (1,), jnp.float32, math.log(2.0), math.log(8.0))), 2.0, 8.0),
        "logit_bias": jnp.clip(jax.random.uniform(key_of[3], (1,), jnp.float32, -8.0, -4.0), -8.0, -4.0),
    }


def pair_terms(images, text_block, image_rows, text_rows, scaling, offset):
    logits = scaling * lax.dot_general(images, text_block, (((1,), (1,)), ((), ())), preferred_element_type=jnp.float32) + offset
    label_sign = jnp.where(image_rows[:, None] == text_rows[None, :], 1.0, -1.0).astype(jnp.float32)
    signed = label_sign * logits
    loss_part = jnp.sum(jax.nn.softplus(-signed))
    weights = (scaling * (-label_sign * jax.nn.sigmoid(-signed))).astype(jnp.bfloat16)
    grad_text = lax.dot_general(weights, images, (((0,), (0,)), ((), ())), preferred_element_type=jnp.float32)
    return loss_part, weights, grad_text


def reference(image_embed, text_embed, logit_scale, logit_bias):
    pair_count = image_embed.shape[0]
    feature_count = image_embed.shape[1]
    block_rows = min(512, pair_count)
    block_total = pair_count // block_rows
    scaling = logit_scale[0]
    offset = logit_bias[0]
    text_rows = jnp.arange(pair_count, dtype=jnp.int32)

    def one_block(state, block_index):
        grad_sum, loss_sum = state
        start = (block_index * block_rows).astype(jnp.int32)
        image_block = lax.dynamic_slice_in_dim(image_embed, start, block_rows, 0)
        image_rows = start + jnp.arange(block_rows, dtype=jnp.int32)
        loss_part, weights, grad_text = pair_terms(image_block, text_embed, image_rows, text_rows, scaling, offset)
        image_part = jnp.dot(weights, text_embed, preferred_element_type=jnp.float32)
        return (grad_sum + grad_text, loss_sum + loss_part), image_part

    start_state = (jnp.zeros((pair_count, feature_count), jnp.float32), jnp.zeros((), jnp.float32))
    (text_grad, loss_sum), image_parts = lax.scan(one_block, start_state, jnp.arange(block_total, dtype=jnp.int32))
    image_grad = image_parts.reshape(pair_count, feature_count)
    loss = (loss_sum / pair_count).reshape(1)
    return (loss, image_grad, text_grad)
```

```python
import functools

import jax
import jax.numpy as jnp
from jax import lax
from jax.experimental import pallas as pl
from jax.experimental.pallas import tpu as pltpu
from jax.sharding import PartitionSpec as P

MESH = pl.DeviceIdType.MESH
F32 = jnp.float32
BF16 = jnp.bfloat16
ROWS = 16
SET = 16 * ROWS
NT = (((1,), (1,)), ((), ()))


def place():
    wide = lax.axis_index("wide")
    narrow = lax.axis_index("narrow")
    return narrow // 4, (wide // 2) % 8, (wide // 16) * 4 + narrow % 4, wide % 2


def device(x, y, z, core):
    return ((z // 4) * 16 + y * 2 + core, x * 4 + z % 4)


def pair_weights(dots, scaling, offset, diagonal):
    logits = scaling * dots + offset
    if diagonal is None:
        turned = logits
    else:
        turned = jnp.where(diagonal, -logits, logits)
    small = jnp.exp(-jnp.abs(turned))
    chance = jnp.where(turned >= 0.0, 1.0, small) / (1.0 + small)
    weights = scaling * chance
    if diagonal is not None:
        weights = jnp.where(diagonal, -weights, weights)
    return turned, small, weights.astype(BF16)


def kernel(
    image_ref,
    text_ref,
    scale_ref,
    bias_ref,
    loss_ref,
    image_grad_ref,
    text_grad_ref,
    images,
    texts,
    weights,
    send_a,
    own_a,
    recv_a,
    send_b,
    recv_b,
    totals,
    first_send,
    first_recv,
    second_send,
    second_recv,
    sibling_send,
    sibling_recv,
    a_send,
    a_recv,
    b_send,
    b_recv,
    loss_send,
    loss_recv,
):
    x, y, z, core = place()
    scaling = scale_ref[0]
    offset = bias_ref[0]

    def along_x(k):
        return device((x + k) % 4, y, z, core)

    def along_y(k):
        return device(x, (y + 2 * k) % 8, z, core)

    def along_z(k):
        return device(x, y, (z + 2 * k) % 8, core)

    def in_block(k):
        flip_y, flip_z = k % 2, k // 2
        yy = y + flip_y * (1 - 2 * (y % 2))
        zz = z + flip_z * (1 - 2 * (z % 2))
        return device(x, yy, zz, core)

    def first_text(k):
        return device(x, (y + 2 * k * (1 - core)) % 8, (z + 2 * k * core) % 8, core)

    def second_text(k):
        return device(x, (y + 2 * k * core) % 8, (z + 2 * k * (1 - core)) % 8, core)

    sibling = device(x, y, z, 1 - core)

    def copy(src, dst, send, recv, to):
        made = pltpu.make_async_remote_copy(
            src_ref=src, dst_ref=dst, send_sem=send, recv_sem=recv, device_id=to, device_id_type=MESH
        )
        made.start()
        return made

    images[0:ROWS] = image_ref[...]
    texts[0:ROWS] = text_ref[...]

    barrier = pltpu.get_barrier_semaphore()
    for k in (1, 2, 3):
        for reach in (along_x, along_y, along_z, in_block):
            pl.semaphore_signal(barrier, inc=1, device_id=reach(k), device_id_type=MESH)
    pl.semaphore_signal(barrier, inc=1, device_id=sibling, device_id_type=MESH)
    pl.semaphore_wait(barrier, 13)

    sent = []
    first = []
    for k in (1, 2, 3):
        first.append(
            copy(
                texts.at[pl.ds(0, ROWS)],
                texts.at[pl.ds((4 - k) * ROWS, ROWS)],
                first_send.at[k - 1],
                first_recv.at[k - 1],
                first_text(k),
            )
        )
    for k in (1, 2, 3):
        first.append(
            copy(
                images.at[pl.ds(0, ROWS)],
                images.at[pl.ds(k * ROWS, ROWS)],
                first_send.at[2 + k],
                first_recv.at[2 + k],
                in_block(k),
            )
        )
    bundle = 4 * ROWS
    second = []
    for part, (array, reach) in enumerate(((images, along_x), (texts, second_text))):
        for made in first[3:] if part == 0 else first[:3]:
            made.wait_recv()
        for k in (1, 2, 3):
            second.append(
                copy(
                    array.at[pl.ds(0, bundle)],
                    array.at[pl.ds((4 - k) * bundle, bundle)],
                    second_send.at[3 * part + k - 1],
                    second_recv.at[3 * part + k - 1],
                    reach(k),
                )
            )
    sent += first + second
    shared = []
    for part, array in enumerate((images, texts)):
        for made in second[3 * part : 3 * part + 3]:
            made.wait_recv()
        shared.append(
            copy(
                array.at[pl.ds(0, SET)],
                array.at[pl.ds(SET, SET)],
                sibling_send.at[part],
                sibling_recv.at[part],
                sibling,
            )
        )
    sent += shared

    rows = lax.broadcasted_iota(jnp.int32, (SET, SET), 0)
    columns = lax.broadcasted_iota(jnp.int32, (SET, SET), 1)
    diagonal = (rows == columns) & (rows < ROWS)

    loss = jnp.zeros((8, 128), F32)
    partial = []
    for part, (mine, other) in enumerate(((images, texts), (texts, images))):
        for half in (0, 1):
            if half == 1:
                shared[1 - part].wait_recv()
            dots = lax.dot_general(
                mine[0:SET], other[half * SET : (half + 1) * SET], NT, preferred_element_type=F32
            )
            turned, small, tile = pair_weights(dots, scaling, offset, diagonal if half == 0 else None)
            weights[:, half * SET : (half + 1) * SET] = tile
            if part == 0:
                terms = jnp.maximum(turned, 0.0) + jnp.log1p(small)
                terms = jnp.sum(terms.reshape(SET // 8, 8, SET), axis=0)
                loss = loss + terms[:, 0:128] + terms[:, 128:256]
        grads = jnp.dot(weights[...], other[...], preferred_element_type=F32)
        own_a[part] = grads[0:bundle]
        send_a[part] = grads[bundle:].astype(BF16)
        reach = along_x if part == 0 else second_text
        for k in (1, 2, 3):
            partial.append(
                copy(
                    send_a.at[part, pl.ds((k - 1) * bundle, bundle)],
                    recv_a.at[part, 3 - k],
                    a_send.at[part, k - 1],
                    a_recv.at[part, k - 1],
                    reach(k),
                )
            )
    sent += partial

    stages = (
        (core, (1,), lambda k: sibling),
        (x, (1, 2, 3), along_x),
        ((y % 2) + 2 * (z % 2), (1, 2, 3), in_block),
        (y // 2, (1, 2, 3), along_y),
        (z // 2, (1, 2, 3), along_z),
    )

    def give(stage, value):
        slot, steps, reach = stages[stage]
        totals[stage, slot] = value
        return [
            copy(
                totals.at[stage, slot],
                totals.at[stage, slot],
                loss_send.at[stage, k - 1],
                loss_recv.at[stage, k - 1],
                reach(k),
            )
            for k in steps
        ]

    def take(stage, gifts):
        for made in gifts:
            made.wait_recv()
        sent.extend(gifts)
        value = totals[stage, 0] + totals[stage, 1]
        if stage > 0:
            value = value + totals[stage, 2] + totals[stage, 3]
        return value

    loss = take(0, give(0, loss))
    gifts = give(1, loss)

    last = []
    for part in (0, 1):
        for made in partial[3 * part : 3 * part + 3]:
            made.wait_recv()
        total = own_a[part]
        for k in range(3):
            total = total + recv_a[part, k].astype(F32)
        send_b[part] = total
        reach = in_block if part == 0 else first_text
        for k in (1, 2, 3):
            last.append(
                copy(
                    send_b.at[part, pl.ds(k * ROWS, ROWS)],
                    recv_b.at[part, k - 1 if part == 0 else 3 - k],
                    b_send.at[part, k - 1],
                    b_recv.at[part, k - 1],
                    reach(k),
                )
            )
        loss = take(1 + part, gifts)
        gifts = give(2 + part, loss)
    loss = take(3, gifts)
    gifts = give(4, loss)
    sent += last
    for part, out in enumerate((image_grad_ref, text_grad_ref)):
        for made in last[3 * part : 3 * part + 3]:
            made.wait_recv()
        total = send_b[part, 0:ROWS]
        for k in range(3):
            total = total + recv_b[part, k]
        out[...] = total
    loss = take(4, gifts)
    loss_ref[0] = jnp.sum(loss) / 8192.0
    for made in sent:
        made.wait_send()


def local(image_embed, text_embed, logit_scale, logit_bias):
    width = image_embed.shape[1]
    vmem = pl.BlockSpec(memory_space=pltpu.VMEM)
    smem = pl.BlockSpec(memory_space=pltpu.SMEM)
    dma = pltpu.SemaphoreType.DMA
    grad = jax.ShapeDtypeStruct((ROWS, width), F32)
    return pl.pallas_call(
        kernel,
        out_shape=(jax.ShapeDtypeStruct((1,), F32), grad, grad),
        in_specs=[vmem, vmem, smem, smem],
        out_specs=(smem, vmem, vmem),
        scratch_shapes=[
            pltpu.VMEM((2 * SET, width), BF16),
            pltpu.VMEM((2 * SET, width), BF16),
            pltpu.VMEM((SET, 2 * SET), BF16),
            pltpu.VMEM((2, 12 * ROWS, width), BF16),
            pltpu.VMEM((2, 4 * ROWS, width), F32),
            pltpu.VMEM((2, 3, 4 * ROWS, width), BF16),
            pltpu.VMEM((2, 4 * ROWS, width), F32),
            pltpu.VMEM((2, 3, ROWS, width), F32),
            pltpu.VMEM((5, 4, 8, 128), F32),
            dma((6,)),
            dma((6,)),
            dma((6,)),
            dma((6,)),
            dma((2,)),
            dma((2,)),
            dma((2, 3)),
            dma((2, 3)),
            dma((2, 3)),
            dma((2, 3)),
            dma((5, 3)),
            dma((5, 3)),
        ],
        compiler_params=pltpu.CompilerParams(
            collective_id=0, has_side_effects=True, vmem_limit_bytes=48 * 2**20
        ),
        name="pairs",
    )(image_embed, text_embed, logit_scale, logit_bias)


def solution(mesh):
    rows = P(("wide", "narrow"), None)
    return jax.shard_map(
        local, mesh=mesh, in_specs=(rows, rows, P(), P()), out_specs=(P(), rows, rows), check_vma=False
    )
```

```python
import jax
import jax.numpy as jnp
from jax import lax
from jax.experimental import pallas as pl
from jax.experimental.pallas import tpu as pltpu
from jax.sharding import PartitionSpec as P

MESH = pl.DeviceIdType.MESH
F32 = jnp.float32
BF16 = jnp.bfloat16
ROWS = 16
SET = 16 * ROWS
CUT = 640
NT = (((1,), (1,)), ((), ()))


def place():
    wide = lax.axis_index("wide")
    narrow = lax.axis_index("narrow")
    return narrow // 4, (wide // 2) % 8, (wide // 16) * 4 + narrow % 4, wide % 2


def device(x, y, z, core):
    return ((z // 4) * 16 + y * 2 + core, x * 4 + z % 4)


def pair_weights(dots, scaling, offset, diagonal):
    logits = scaling * dots + offset
    if diagonal is None:
        turned = logits
    else:
        turned = jnp.where(diagonal, -logits, logits)
    small = jnp.exp(-jnp.abs(turned))
    chance = jnp.where(turned >= 0.0, 1.0, small) / (1.0 + small)
    weights = scaling * chance
    if diagonal is not None:
        weights = jnp.where(diagonal, -weights, weights)
    return turned, small, weights.astype(BF16)


def kernel(
    image_ref,
    text_ref,
    scale_ref,
    bias_ref,
    loss_ref,
    image_grad_ref,
    text_grad_ref,
    images,
    texts,
    weights,
    text_parts,
    text_near,
    text_far,
    text_own,
    came_z,
    came_y,
    last_y,
    last_z,
    image_parts,
    image_own,
    came_x,
    block_parts,
    last_block,
    totals,
    load,
    near_send,
    near_recv,
    far_send,
    far_recv,
    image_send,
    image_recv,
    sibling_send,
    sibling_recv,
    a_send,
    a_recv,
    b_send,
    b_recv,
    image_a_send,
    image_a_recv,
    image_b_send,
    image_b_recv,
    loss_send,
    loss_recv,
):
    x, y, z, core = place()
    steps = (2, 1, 3)

    def along_x(k):
        return device((x + k) % 4, y, z, core)

    def along_y(k):
        return device(x, (y + 2 * k) % 8, z, core)

    def along_z(k):
        return device(x, y, (z + 2 * k) % 8, core)

    def in_block(k):
        flip_y, flip_z = k % 2, k // 2
        yy = y + flip_y * (1 - 2 * (y % 2))
        zz = z + flip_z * (1 - 2 * (z % 2))
        return device(x, yy, zz, core)

    sibling = device(x, y, z, 1 - core)

    sent = []

    def copy(src, dst, send, recv, to):
        made = pltpu.make_async_remote_copy(
            src_ref=src, dst_ref=dst, send_sem=send, recv_sem=recv, device_id=to, device_id_type=MESH
        )
        made.start()
        sent.append(made)
        return made

    def arrived(copies):
        for made in copies:
            made.wait_recv()

    loads = [
        pltpu.make_async_copy(text_ref, texts.at[0, 0, 0], load.at[0]),
        pltpu.make_async_copy(image_ref, images.at[pl.ds(0, ROWS)], load.at[1]),
    ]
    for made in loads:
        made.start()
    barrier = pltpu.get_barrier_semaphore()
    for k in steps:
        for reach in (along_y, along_z, along_x, in_block):
            pl.semaphore_signal(barrier, inc=1, device_id=reach(k), device_id_type=MESH)
    pl.semaphore_signal(barrier, inc=1, device_id=sibling, device_id_type=MESH)
    scaling = scale_ref[0]
    offset = bias_ref[0]
    for made in loads:
        made.wait()
    pl.semaphore_wait(barrier, 13)

    from_y, from_z, from_block = [], [], []
    mine = texts.at[0, 0, 0]
    for k in steps:
        from_y.append(copy(mine, texts.at[0, 0, 4 - k], near_send.at[0, k - 1], near_recv.at[0, k - 1], along_y(k)))
        from_z.append(copy(mine, texts.at[0, 4 - k, 0], near_send.at[1, k - 1], near_recv.at[1, k - 1], along_z(k)))
    own = images.at[pl.ds(0, ROWS)]
    for k in steps:
        from_block.append(
            copy(own, images.at[pl.ds(k * ROWS, ROWS)], image_send.at[0, k - 1], image_recv.at[0, k - 1], in_block(k))
        )
    arrived(from_block)
    from_x = []
    bundle = 4 * ROWS
    for k in steps:
        from_x.append(
            copy(
                images.at[pl.ds(0, bundle)],
                images.at[pl.ds((4 - k) * bundle, bundle)],
                image_send.at[1, k - 1],
                image_recv.at[1, k - 1],
                along_x(k),
            )
        )
    head, tail = pl.ds(0, CUT), pl.ds(CUT, texts.shape[-1] - CUT)
    rest = pl.ds(1, 3)
    arrived(from_y)
    passed = []
    for k in steps:
        passed.append(
            copy(
                texts.at[0, 0, rest, :, head],
                texts.at[0, 4 - k, rest, :, head],
                far_send.at[0, k - 1],
                far_recv.at[0, k - 1],
                along_z(k),
            )
        )
    arrived(from_z)
    for k in steps:
        passed.append(
            copy(
                texts.at[0, rest, 0, :, tail],
                texts.at[0, rest, 4 - k, :, tail],
                far_send.at[1, k - 1],
                far_recv.at[1, k - 1],
                along_y(k),
            )
        )
    arrived(from_x)
    image_share = copy(
        images.at[pl.ds(0, SET)], images.at[pl.ds(SET, SET)], sibling_send.at[0], sibling_recv.at[0], sibling
    )
    arrived(passed)
    text_share = copy(texts.at[0], texts.at[1], sibling_send.at[1], sibling_recv.at[1], sibling)

    rows = lax.broadcasted_iota(jnp.int32, (SET, SET), 0)
    columns = lax.broadcasted_iota(jnp.int32, (SET, SET), 1)
    diagonal = (rows == columns) & (rows < ROWS)

    stages = (
        (core, (1,), lambda k: sibling),
        (x, steps, along_x),
        ((y % 2) + 2 * (z % 2), steps, in_block),
        (y // 2, steps, along_y),
        (z // 2, steps, along_z),
    )

    def give(stage, value):
        slot, ways, reach = stages[stage]
        totals[stage, slot] = value
        return [
            copy(
                totals.at[stage, slot],
                totals.at[stage, slot],
                loss_send.at[stage, k - 1],
                loss_recv.at[stage, k - 1],
                reach(k),
            )
            for k in ways
        ]

    def take(stage, gifts):
        arrived(gifts)
        value = totals[stage, 0] + totals[stage, 1]
        if stage > 0:
            value = value + totals[stage, 2] + totals[stage, 3]
        return value

    def text_set(half):
        return texts[half].reshape(SET, texts.shape[-1])

    loss = jnp.zeros((8, 128), F32)
    for half in (0, 1):
        if half == 1:
            image_share.wait_recv()
        dots = lax.dot_general(
            text_set(0), images[half * SET : (half + 1) * SET], NT, preferred_element_type=F32
        )
        turned, small, tile = pair_weights(dots, scaling, offset, diagonal if half == 0 else None)
        weights[:, half * SET : (half + 1) * SET] = tile
        terms = jnp.maximum(turned, 0.0) + jnp.log1p(small)
        terms = jnp.sum(terms.reshape(SET // 8, 8, SET), axis=0)
        loss = loss + terms[:, 0:128] + terms[:, 128:256]
    gifts = give(0, loss)
    grads = jnp.dot(weights[...], images[...], preferred_element_type=F32).reshape(4, 4, ROWS, -1)
    text_parts[...] = grads.astype(BF16)
    text_near[...] = grads[0, 1:4, :, 0:CUT]
    text_far[...] = grads[1:4, 0, :, CUT:]
    text_own[...] = grads[0, 0]
    to_z, to_y = [], []
    for k in steps:
        to_z.append(
            copy(
                text_parts.at[k, rest, :, head], came_z.at[3 - k], a_send.at[0, k - 1], a_recv.at[0, k - 1], along_z(k)
            )
        )
        to_y.append(
            copy(
                text_parts.at[rest, k, :, tail], came_y.at[3 - k], a_send.at[1, k - 1], a_recv.at[1, k - 1], along_y(k)
            )
        )
    gifts = give(1, take(0, gifts))

    text_share.wait_recv()
    for half in (0, 1):
        dots = lax.dot_general(images[0:SET], text_set(half), NT, preferred_element_type=F32)
        weights[:, half * SET : (half + 1) * SET] = pair_weights(
            dots, scaling, offset, diagonal if half == 0 else None
        )[2]
    grads = jnp.dot(
        weights[...], texts[...].reshape(2 * SET, texts.shape[-1]), preferred_element_type=F32
    )
    image_own[...] = grads[0:bundle]
    image_parts[...] = grads[bundle:].astype(BF16)
    to_x = []
    for k in steps:
        to_x.append(
            copy(
                image_parts.at[pl.ds((k - 1) * bundle, bundle)],
                came_x.at[3 - k],
                image_a_send.at[k - 1],
                image_a_recv.at[k - 1],
                along_x(k),
            )
        )
    gifts = give(2, take(1, gifts))

    arrived(to_z)
    total = text_near[...]
    for k in range(3):
        total = total + came_z[k].astype(F32)
    text_parts[0, 1:4, :, 0:CUT] = total.astype(BF16)
    out_y, out_z, out_block = [], [], []
    for k in steps:
        out_y.append(
            copy(text_parts.at[0, k], last_y.at[3 - k], b_send.at[0, k - 1], b_recv.at[0, k - 1], along_y(k))
        )
    arrived(to_y)
    total = text_far[...]
    for k in range(3):
        total = total + came_y[k].astype(F32)
    text_parts[1:4, 0, :, CUT:] = total.astype(BF16)
    for k in steps:
        out_z.append(
            copy(text_parts.at[k, 0], last_z.at[3 - k], b_send.at[1, k - 1], b_recv.at[1, k - 1], along_z(k))
        )
    gifts = give(3, take(2, gifts))
    arrived(to_x)
    total = image_own[...]
    for k in range(3):
        total = total + came_x[k].astype(F32)
    image_own[0:ROWS] = total[0:ROWS]
    block_parts[...] = total[ROWS:].astype(BF16)
    for k in steps:
        out_block.append(
            copy(
                block_parts.at[pl.ds((k - 1) * ROWS, ROWS)],
                last_block.at[k - 1],
                image_b_send.at[k - 1],
                image_b_recv.at[k - 1],
                in_block(k),
            )
        )
    gifts = give(4, take(3, gifts))
    arrived(out_block)
    total = image_own[0:ROWS]
    for k in range(3):
        total = total + last_block[k].astype(F32)
    image_grad_ref[...] = total
    arrived(out_y + out_z)
    total = text_own[...]
    for k in range(3):
        total = total + last_y[k].astype(F32) + last_z[k].astype(F32)
    text_grad_ref[...] = total
    loss_ref[0] = jnp.sum(take(4, gifts)) / 8192.0
    for made in sent:
        made.wait_send()


def local(image_embed, text_embed, logit_scale, logit_bias):
    width = image_embed.shape[1]
    vmem = pl.BlockSpec(memory_space=pltpu.VMEM)
    smem = pl.BlockSpec(memory_space=pltpu.SMEM)
    hbm = pl.BlockSpec(memory_space=pltpu.HBM)
    dma = pltpu.SemaphoreType.DMA
    grad = jax.ShapeDtypeStruct((ROWS, width), F32)
    return pl.pallas_call(
        kernel,
        out_shape=(jax.ShapeDtypeStruct((1,), F32), grad, grad),
        in_specs=[hbm, hbm, smem, smem],
        out_specs=(smem, vmem, vmem),
        scratch_shapes=[
            pltpu.VMEM((2 * SET, width), BF16),
            pltpu.VMEM((2, 4, 4, ROWS, width), BF16),
            pltpu.VMEM((SET, 2 * SET), BF16),
            pltpu.VMEM((4, 4, ROWS, width), BF16),
            pltpu.VMEM((3, ROWS, CUT), F32),
            pltpu.VMEM((3, ROWS, width - CUT), F32),
            pltpu.VMEM((ROWS, width), F32),
            pltpu.VMEM((3, 3, ROWS, CUT), BF16),
            pltpu.VMEM((3, 3, ROWS, width - CUT), BF16),
            pltpu.VMEM((3, ROWS, width), BF16),
            pltpu.VMEM((3, ROWS, width), BF16),
            pltpu.VMEM((12 * ROWS, width), BF16),
            pltpu.VMEM((4 * ROWS, width), F32),
            pltpu.VMEM((3, 4 * ROWS, width), BF16),
            pltpu.VMEM((3 * ROWS, width), BF16),
            pltpu.VMEM((3, ROWS, width), BF16),
            pltpu.VMEM((5, 4, 8, 128), F32),
            dma((2,)),
            dma((2, 3)),
            dma((2, 3)),
            dma((2, 3)),
            dma((2, 3)),
            dma((2, 3)),
            dma((2, 3)),
            dma((2,)),
            dma((2,)),
            dma((2, 3)),
            dma((2, 3)),
            dma((2, 3)),
            dma((2, 3)),
            dma((3,)),
            dma((3,)),
            dma((3,)),
            dma((3,)),
            dma((5, 3)),
            dma((5, 3)),
        ],
        compiler_params=pltpu.CompilerParams(
            collective_id=0, has_side_effects=True, vmem_limit_bytes=60 * 2**20
        ),
        name="pairs",
    )(image_embed, text_embed, logit_scale, logit_bias)


def solution(mesh):
    rows = P(("wide", "narrow"), None)
    return jax.shard_map(
        local, mesh=mesh, in_specs=(rows, rows, P(), P()), out_specs=(P(), rows, rows), check_vma=False
    )
```

```python
import jax
import jax.numpy as jnp
from jax import lax
from jax.experimental import pallas as pl
from jax.experimental.pallas import tpu as pltpu
from jax.sharding import PartitionSpec as P

MESH = pl.DeviceIdType.MESH
F32 = jnp.float32
BF16 = jnp.bfloat16
ROWS = 16
SET = 16 * ROWS
CUT = 640
NT = (((1,), (1,)), ((), ()))


def place():
    wide = lax.axis_index("wide")
    narrow = lax.axis_index("narrow")
    y = lax.rem(lax.div(wide, 2), 8)
    z = lax.div(wide, 16) * 4 + lax.rem(narrow, 4)
    return lax.div(narrow, 4), y, z, lax.rem(wide, 2)


def device(x, y, z, core):
    return (lax.div(z, 4) * 16 + y * 2 + core, x * 4 + lax.rem(z, 4))


def pair_weights(dots, scaling, offset, diagonal):
    logits = scaling * dots + offset
    if diagonal is None:
        turned = logits
    else:
        turned = jnp.where(diagonal, -logits, logits)
    small = jnp.exp(-jnp.abs(turned))
    chance = jnp.where(turned >= 0.0, 1.0, small) / (1.0 + small)
    weights = scaling * chance
    if diagonal is not None:
        weights = jnp.where(diagonal, -weights, weights)
    return turned, small, weights.astype(BF16)


def kernel(
    image_ref,
    text_ref,
    scale_ref,
    bias_ref,
    loss_ref,
    image_grad_ref,
    text_grad_ref,
    images,
    texts,
    weights,
    text_parts,
    text_near,
    text_far,
    text_own,
    came_z,
    came_y,
    last_y,
    last_z,
    image_parts,
    image_own,
    came_x,
    block_parts,
    last_block,
    totals,
    numbers,
    load,
    near_send,
    near_recv,
    far_send,
    far_recv,
    image_send,
    image_recv,
    sibling_send,
    sibling_recv,
    a_send,
    a_recv,
    b_send,
    b_recv,
    image_a_send,
    image_a_recv,
    image_b_send,
    image_b_recv,
    loss_send,
    loss_recv,
):
    x, y, z, core = place()
    steps = (2, 1, 3)

    flipped_y = y + 1 - 2 * lax.rem(y, 2)
    flipped_z = z + 1 - 2 * lax.rem(z, 2)
    all_steps = (4, 3, 5, 2, 6, 1, 7)

    def along_x(k):
        return device(lax.rem(x + k, 4), y, z, core)

    def ring_y(k):
        return device(x, lax.rem(y + k, 8), z, core)

    def ring_z(k):
        return device(x, y, lax.rem(z + k, 8), core)

    def along_y(k):
        return ring_y(2 * k)

    def along_z(k):
        return ring_z(2 * k)

    def in_row(k):
        return device(lax.rem(x + k // 2, 4), y, z, 1 - core if k % 2 else core)

    def in_block(k):
        return device(x, flipped_y if k % 2 else y, flipped_z if k // 2 else z, core)

    sibling = in_row(1)

    sent = []

    def copy(src, dst, send, recv, to):
        made = pltpu.make_async_remote_copy(
            src_ref=src, dst_ref=dst, send_sem=send, recv_sem=recv, device_id=to, device_id_type=MESH
        )
        made.start()
        sent.append(made)
        return made

    def arrived(copies):
        for made in copies:
            made.wait_recv()

    barrier = pltpu.get_barrier_semaphore()
    for reach in (ring_y, ring_z, in_row):
        for k in all_steps:
            pl.semaphore_signal(barrier, inc=1, device_id=reach(k), device_id_type=MESH)
    pl.semaphore_signal(barrier, inc=1, device_id=in_block(3), device_id_type=MESH)
    loads = [
        pltpu.make_async_copy(image_ref, images.at[pl.ds(0, ROWS)], load.at[0]),
        pltpu.make_async_copy(text_ref, texts.at[0, 0, 0], load.at[1]),
        pltpu.make_async_copy(scale_ref, numbers.at[0], load.at[2]),
        pltpu.make_async_copy(bias_ref, numbers.at[1], load.at[3]),
    ]
    for made in loads:
        made.start()
    for made in loads:
        made.wait()
    scaling = numbers[0, 0]
    offset = numbers[1, 0]
    pl.semaphore_wait(barrier, 22)

    from_y, from_z, from_block = [], [], []
    own = images.at[pl.ds(0, ROWS)]
    for k in steps:
        from_block.append(
            copy(own, images.at[pl.ds(k * ROWS, ROWS)], image_send.at[0, k - 1], image_recv.at[0, k - 1], in_block(k))
        )
    mine = texts.at[0, 0, 0]
    for k in steps:
        from_y.append(copy(mine, texts.at[0, 0, 4 - k], near_send.at[0, k - 1], near_recv.at[0, k - 1], along_y(k)))
        from_z.append(copy(mine, texts.at[0, 4 - k, 0], near_send.at[1, k - 1], near_recv.at[1, k - 1], along_z(k)))
    arrived(from_block)
    from_x = []
    bundle = 4 * ROWS
    for k in steps:
        from_x.append(
            copy(
                images.at[pl.ds(0, bundle)],
                images.at[pl.ds((4 - k) * bundle, bundle)],
                image_send.at[1, k - 1],
                image_recv.at[1, k - 1],
                along_x(k),
            )
        )
    head, tail = pl.ds(0, CUT), pl.ds(CUT, texts.shape[-1] - CUT)
    rest = pl.ds(1, 3)
    arrived(from_y)
    passed = []
    for k in steps:
        passed.append(
            copy(
                texts.at[0, 0, rest, :, head],
                texts.at[0, 4 - k, rest, :, head],
                far_send.at[0, k - 1],
                far_recv.at[0, k - 1],
                along_z(k),
            )
        )
    arrived(from_z)
    for k in steps:
        passed.append(
            copy(
                texts.at[0, rest, 0, :, tail],
                texts.at[0, rest, 4 - k, :, tail],
                far_send.at[1, k - 1],
                far_recv.at[1, k - 1],
                along_y(k),
            )
        )
    arrived(from_x)
    image_share = copy(
        images.at[pl.ds(0, SET)], images.at[pl.ds(SET, SET)], sibling_send.at[0], sibling_recv.at[0], sibling
    )
    arrived(passed)
    text_share = copy(texts.at[0], texts.at[1], sibling_send.at[1], sibling_recv.at[1], sibling)

    rows = lax.broadcasted_iota(jnp.int32, (SET, SET), 0)
    columns = lax.broadcasted_iota(jnp.int32, (SET, SET), 1)
    diagonal = (rows == columns) & (rows < ROWS)

    stages = ((y, ring_y), (z, ring_z), (2 * x + core, in_row))

    def way_back(stage, k):
        return 8 - k if stage < 2 else (8 - k // 2 * 2) % 8 + k % 2

    def give(stage, value):
        slot, reach = stages[stage]
        totals[stage, slot] = value
        return [
            copy(
                totals.at[stage, slot],
                totals.at[stage, slot],
                loss_send.at[stage, k - 1],
                loss_recv.at[stage, way_back(stage, k) - 1],
                reach(k),
            )
            for k in all_steps
        ]

    def take(stage, gifts):
        arrived(gifts)
        value = totals[stage, 0]
        for k in range(1, 8):
            value = value + totals[stage, k]
        return value

    def text_set(half):
        return texts[half].reshape(SET, texts.shape[-1])

    loss = jnp.zeros((8, 128), F32)
    for half in (0, 1):
        if half == 1:
            image_share.wait_recv()
        dots = lax.dot_general(
            text_set(0), images[half * SET : (half + 1) * SET], NT, preferred_element_type=F32
        )
        turned, small, tile = pair_weights(dots, scaling, offset, diagonal if half == 0 else None)
        weights[:, half * SET : (half + 1) * SET] = tile
        terms = jnp.maximum(turned, 0.0) + jnp.log1p(small)
        terms = jnp.sum(terms.reshape(SET // 8, 8, SET), axis=0)
        loss = loss + terms[:, 0:128] + terms[:, 128:256]
    gifts = give(0, loss)
    grads = jnp.dot(weights[...], images[...], preferred_element_type=F32).reshape(4, 4, ROWS, -1)
    text_parts[...] = grads.astype(BF16)
    text_near[...] = grads[0, 1:4, :, 0:CUT]
    text_far[...] = grads[1:4, 0, :, CUT:]
    text_own[...] = grads[0, 0]
    to_z, to_y = [], []
    for k in steps:
        to_z.append(
            copy(
                text_parts.at[k, rest, :, head], came_z.at[3 - k], a_send.at[0, k - 1], a_recv.at[0, k - 1], along_z(k)
            )
        )
        to_y.append(
            copy(
                text_parts.at[rest, k, :, tail], came_y.at[3 - k], a_send.at[1, k - 1], a_recv.at[1, k - 1], along_y(k)
            )
        )

    text_share.wait_recv()
    for half in (0, 1):
        dots = lax.dot_general(images[0:SET], text_set(half), NT, preferred_element_type=F32)
        weights[:, half * SET : (half + 1) * SET] = pair_weights(
            dots, scaling, offset, diagonal if half == 0 else None
        )[2]
    grads = jnp.dot(
        weights[...], texts[...].reshape(2 * SET, texts.shape[-1]), preferred_element_type=F32
    )
    image_own[...] = grads[0:bundle]
    image_parts[...] = grads[bundle:].astype(BF16)
    to_x = []
    for k in steps:
        to_x.append(
            copy(
                image_parts.at[pl.ds((k - 1) * bundle, bundle)],
                came_x.at[3 - k],
                image_a_send.at[k - 1],
                image_a_recv.at[k - 1],
                along_x(k),
            )
        )
    gifts = give(1, take(0, gifts))

    arrived(to_z)
    total = text_near[...]
    for k in range(3):
        total = total + came_z[k].astype(F32)
    text_parts[0, 1:4, :, 0:CUT] = total.astype(BF16)
    out_y, out_z, out_block = [], [], []
    for k in steps:
        out_y.append(
            copy(text_parts.at[0, k], last_y.at[3 - k], b_send.at[0, k - 1], b_recv.at[0, k - 1], along_y(k))
        )
    arrived(to_y)
    total = text_far[...]
    for k in range(3):
        total = total + came_y[k].astype(F32)
    text_parts[1:4, 0, :, CUT:] = total.astype(BF16)
    for k in steps:
        out_z.append(
            copy(text_parts.at[k, 0], last_z.at[3 - k], b_send.at[1, k - 1], b_recv.at[1, k - 1], along_z(k))
        )
    gifts = give(2, take(1, gifts))
    arrived(to_x)
    total = image_own[...]
    for k in range(3):
        total = total + came_x[k].astype(F32)
    image_own[0:ROWS] = total[0:ROWS]
    block_parts[...] = total[ROWS:].astype(BF16)
    for k in steps:
        out_block.append(
            copy(
                block_parts.at[pl.ds((k - 1) * ROWS, ROWS)],
                last_block.at[k - 1],
                image_b_send.at[k - 1],
                image_b_recv.at[k - 1],
                in_block(k),
            )
        )
    arrived(out_block)
    total = image_own[0:ROWS]
    for k in range(3):
        total = total + last_block[k].astype(F32)
    image_grad_ref[...] = total
    arrived(out_y + out_z)
    total = text_own[...]
    for k in range(3):
        total = total + last_y[k].astype(F32) + last_z[k].astype(F32)
    text_grad_ref[...] = total
    loss_ref[...] = jnp.full(loss_ref.shape, jnp.sum(take(2, gifts)) / 8192.0, F32)
    for made in sent:
        made.wait_send()


def local(image_embed, text_embed, logit_scale, logit_bias):
    width = image_embed.shape[1]
    vmem = pl.BlockSpec(memory_space=pltpu.VMEM)
    hbm = pl.BlockSpec(memory_space=pltpu.HBM)
    dma = pltpu.SemaphoreType.DMA
    grad = jax.ShapeDtypeStruct((ROWS, width), F32)
    loss, image_grad, text_grad = pl.pallas_call(
        kernel,
        out_shape=(jax.ShapeDtypeStruct((8, 128), F32), grad, grad),
        in_specs=[hbm, hbm, hbm, hbm],
        out_specs=(vmem, vmem, vmem),
        scratch_shapes=[
            pltpu.VMEM((2 * SET, width), BF16),
            pltpu.VMEM((2, 4, 4, ROWS, width), BF16),
            pltpu.VMEM((SET, 2 * SET), BF16),
            pltpu.VMEM((4, 4, ROWS, width), BF16),
            pltpu.VMEM((3, ROWS, CUT), F32),
            pltpu.VMEM((3, ROWS, width - CUT), F32),
            pltpu.VMEM((ROWS, width), F32),
            pltpu.VMEM((3, 3, ROWS, CUT), BF16),
            pltpu.VMEM((3, 3, ROWS, width - CUT), BF16),
            pltpu.VMEM((3, ROWS, width), BF16),
            pltpu.VMEM((3, ROWS, width), BF16),
            pltpu.VMEM((12 * ROWS, width), BF16),
            pltpu.VMEM((4 * ROWS, width), F32),
            pltpu.VMEM((3, 4 * ROWS, width), BF16),
            pltpu.VMEM((3 * ROWS, width), BF16),
            pltpu.VMEM((3, ROWS, width), BF16),
            pltpu.VMEM((3, 8, 8, 128), F32),
            pltpu.SMEM((2, 1), F32),
            dma((4,)),
            dma((2, 3)),
            dma((2, 3)),
            dma((2, 3)),
            dma((2, 3)),
            dma((2, 3)),
            dma((2, 3)),
            dma((2,)),
            dma((2,)),
            dma((2, 3)),
            dma((2, 3)),
            dma((2, 3)),
            dma((2, 3)),
            dma((3,)),
            dma((3,)),
            dma((3,)),
            dma((3,)),
            dma((3, 7)),
            dma((3, 7)),
        ],
        compiler_params=pltpu.CompilerParams(
            collective_id=0, has_side_effects=True, vmem_limit_bytes=48 * 2**20
        ),
        name="pairs",
    )(*(pltpu.with_memory_space_constraint(a, pltpu.HBM) for a in (image_embed, text_embed)), logit_scale, logit_bias)

    return loss[0, 0:1], image_grad, text_grad


def solution(mesh):
    rows = P(("wide", "narrow"), None)
    return jax.shard_map(
        local, mesh=mesh, in_specs=(rows, rows, P(), P()), out_specs=(P(), rows, rows), check_vma=False
    )
```

```python
import jax
import jax.numpy as jnp
from jax import lax
from jax.experimental import pallas as pl
from jax.experimental.pallas import tpu as pltpu
from jax.sharding import PartitionSpec as P

MESH = pl.DeviceIdType.MESH
F32 = jnp.float32
BF16 = jnp.bfloat16
ROWS = 16
SET = 16 * ROWS
CUT = 640
NT = (((1,), (1,)), ((), ()))


def place():
    wide = lax.axis_index("wide")
    narrow = lax.axis_index("narrow")
    y = lax.rem(lax.div(wide, 2), 8)
    z = lax.div(wide, 16) * 4 + lax.rem(narrow, 4)
    return lax.div(narrow, 4), y, z, lax.rem(wide, 2)


def device(x, y, z, core):
    return (lax.div(z, 4) * 16 + y * 2 + core, x * 4 + lax.rem(z, 4))


def pair_weights(dots, scaling, offset, diagonal):
    logits = scaling * dots + offset
    if diagonal is None:
        turned = logits
    else:
        turned = jnp.where(diagonal, -logits, logits)
    small = jnp.exp(-jnp.abs(turned))
    chance = jnp.where(turned >= 0.0, 1.0, small) / (1.0 + small)
    weights = scaling * chance
    if diagonal is not None:
        weights = jnp.where(diagonal, -weights, weights)
    return turned, small, weights.astype(BF16)


def kernel(
    image_ref,
    text_ref,
    scale_ref,
    bias_ref,
    loss_ref,
    image_grad_ref,
    text_grad_ref,
    images,
    texts,
    weights,
    text_parts,
    text_near,
    text_far,
    text_own,
    came_z,
    came_y,
    last_y,
    last_z,
    image_parts,
    image_own,
    came_x,
    block_parts,
    last_block,
    totals,
    numbers,
    load,
    send,
    recv,
):
    x, y, z, core = place()
    steps = (2, 1, 3)
    flipped_y = y + 1 - 2 * lax.rem(y, 2)
    flipped_z = z + 1 - 2 * lax.rem(z, 2)
    all_steps = (4, 3, 5, 2, 6, 1, 7)

    def along_x(k):
        return device(lax.rem(x + k, 4), y, z, core)

    def ring_y(k):
        return device(x, lax.rem(y + k, 8), z, core)

    def ring_z(k):
        return device(x, y, lax.rem(z + k, 8), core)

    def along_y(k):
        return ring_y(2 * k)

    def along_z(k):
        return ring_z(2 * k)

    def in_row(k):
        return device(lax.rem(x + k // 2, 4), y, z, 1 - core if k % 2 else core)

    def in_block(k):
        return device(x, flipped_y if k % 2 else y, flipped_z if k // 2 else z, core)

    barrier = pltpu.get_barrier_semaphore()
    for reach in (ring_y, ring_z, in_row):
        for k in all_steps:
            pl.semaphore_signal(barrier, inc=1, device_id=reach(k), device_id_type=MESH)
    pl.semaphore_signal(barrier, inc=1, device_id=in_block(3), device_id_type=MESH)
    loads = [
        pltpu.make_async_copy(image_ref, images.at[pl.ds(0, ROWS)], load.at[0]),
        pltpu.make_async_copy(text_ref, texts.at[0, 0, 0], load.at[1]),
        pltpu.make_async_copy(scale_ref, numbers.at[0], load.at[2]),
        pltpu.make_async_copy(bias_ref, numbers.at[1], load.at[3]),
    ]
    for made in loads:
        made.start()
    for made in loads:
        made.wait()
    scaling = numbers[0, 0]
    offset = numbers[1, 0]
    pl.semaphore_wait(barrier, 22)

    groups = []

    def start(whole, copies):
        group = len(groups)
        groups.append(whole)
        for src, dst, to in copies:
            pltpu.make_async_remote_copy(
                src_ref=src,
                dst_ref=dst,
                send_sem=send.at[group],
                recv_sem=recv.at[group],
                device_id=to,
                device_id_type=MESH,
            ).start()
        return group

    def arrived(*which):
        for group in which:
            pltpu.make_async_copy(groups[group], groups[group], recv.at[group]).wait()

    rest = pl.ds(1, 3)
    head, tail = pl.ds(0, CUT), pl.ds(CUT, texts.shape[-1] - CUT)
    bundle = 4 * ROWS
    own = images.at[pl.ds(0, ROWS)]
    from_block = start(
        images.at[pl.ds(ROWS, 3 * ROWS)],
        [(own, images.at[pl.ds(k * ROWS, ROWS)], in_block(k)) for k in (3, 1, 2)],
    )

    def own_text(part, reach, along_near):
        src = texts.at[0, 0, 0, :, part]
        whole = texts.at[0, 0, rest, :, part] if along_near else texts.at[0, rest, 0, :, part]
        return start(
            whole,
            [
                (src, texts.at[0, 0, 4 - k, :, part] if along_near else texts.at[0, 4 - k, 0, :, part], reach(k))
                for k in steps
            ],
        )

    head_y = own_text(head, along_y, True)
    tail_z = own_text(tail, along_z, False)
    tail_y = own_text(tail, along_y, True)
    head_z = own_text(head, along_z, False)
    arrived(from_block)
    from_x = start(
        images.at[pl.ds(bundle, 3 * bundle)],
        [
            (images.at[pl.ds(0, bundle)], images.at[pl.ds((4 - k) * bundle, bundle)], along_x(k))
            for k in steps
        ],
    )
    arrived(head_y)
    passed_z = start(
        texts.at[0, rest, rest, :, head],
        [(texts.at[0, 0, rest, :, head], texts.at[0, 4 - k, rest, :, head], along_z(k)) for k in steps],
    )
    arrived(tail_z)
    passed_y = start(
        texts.at[0, rest, rest, :, tail],
        [(texts.at[0, rest, 0, :, tail], texts.at[0, rest, 4 - k, :, tail], along_y(k)) for k in steps],
    )
    arrived(from_x)
    image_share = start(
        images.at[pl.ds(SET, SET)], [(images.at[pl.ds(0, SET)], images.at[pl.ds(SET, SET)], in_row(1))]
    )
    arrived(tail_y, head_z, passed_z, passed_y)
    text_share = start(texts.at[1], [(texts.at[0], texts.at[1], in_row(1))])

    rows = lax.broadcasted_iota(jnp.int32, (SET, SET), 0)
    columns = lax.broadcasted_iota(jnp.int32, (SET, SET), 1)
    diagonal = (rows == columns) & (rows < ROWS)

    stages = ((y, ring_y), (z, ring_z), (2 * x + core, in_row))

    def give(stage, value):
        slot, reach = stages[stage]
        totals[stage, slot] = value
        mine = totals.at[stage, slot]
        return start(totals.at[stage, pl.ds(0, 7)], [(mine, mine, reach(k)) for k in all_steps])

    def take(stage, gifts):
        arrived(gifts)
        value = totals[stage, 0]
        for k in range(1, 8):
            value = value + totals[stage, k]
        return value

    def text_set(half):
        return texts[half].reshape(SET, texts.shape[-1])

    loss = jnp.zeros((8, 128), F32)
    for half in (0, 1):
        if half == 1:
            arrived(image_share)
        dots = lax.dot_general(
            text_set(0), images[half * SET : (half + 1) * SET], NT, preferred_element_type=F32
        )
        turned, small, tile = pair_weights(dots, scaling, offset, diagonal if half == 0 else None)
        weights[:, half * SET : (half + 1) * SET] = tile
        terms = jnp.maximum(turned, 0.0) + jnp.log1p(small)
        terms = jnp.sum(terms.reshape(SET // 8, 8, SET), axis=0)
        loss = loss + terms[:, 0:128] + terms[:, 128:256]
    gifts = give(0, loss)
    grads = jnp.dot(weights[...], images[...], preferred_element_type=F32).reshape(4, 4, ROWS, -1)
    text_parts[...] = grads.astype(BF16)
    text_near[...] = grads[0, 1:4, :, 0:CUT]
    text_far[...] = grads[1:4, 0, :, CUT:]
    text_own[...] = grads[0, 0]
    to_z = start(came_z, [(text_parts.at[k, rest, :, head], came_z.at[3 - k], along_z(k)) for k in steps])
    to_y = start(came_y, [(text_parts.at[rest, k, :, tail], came_y.at[3 - k], along_y(k)) for k in steps])

    arrived(text_share)
    for half in (0, 1):
        dots = lax.dot_general(images[0:SET], text_set(half), NT, preferred_element_type=F32)
        weights[:, half * SET : (half + 1) * SET] = pair_weights(
            dots, scaling, offset, diagonal if half == 0 else None
        )[2]
    grads = jnp.dot(
        weights[...], texts[...].reshape(2 * SET, texts.shape[-1]), preferred_element_type=F32
    )
    image_own[...] = grads[0:bundle]
    image_parts[...] = grads[bundle:].astype(BF16)
    to_x = start(
        came_x,
        [(image_parts.at[pl.ds((k - 1) * bundle, bundle)], came_x.at[3 - k], along_x(k)) for k in steps],
    )
    gifts = give(1, take(0, gifts))

    arrived(to_z)
    total = text_near[...]
    for k in range(3):
        total = total + came_z[k].astype(F32)
    text_parts[0, 1:4, :, 0:CUT] = total.astype(BF16)
    out_y = start(last_y, [(text_parts.at[0, k], last_y.at[3 - k], along_y(k)) for k in steps])
    arrived(to_y)
    total = text_far[...]
    for k in range(3):
        total = total + came_y[k].astype(F32)
    text_parts[1:4, 0, :, CUT:] = total.astype(BF16)
    out_z = start(last_z, [(text_parts.at[k, 0], last_z.at[3 - k], along_z(k)) for k in steps])
    arrived(to_x)
    total = image_own[...]
    for k in range(3):
        total = total + came_x[k].astype(F32)
    image_own[0:ROWS] = total[0:ROWS]
    block_parts[...] = total[ROWS:].astype(BF16)
    out_block = start(
        last_block,
        [
            (block_parts.at[pl.ds((k - 1) * ROWS, ROWS)], last_block.at[k - 1], in_block(k))
            for k in (3, 1, 2)
        ],
    )
    gifts = give(2, take(1, gifts))
    arrived(out_y, out_z)
    total = text_own[...]
    for k in range(3):
        total = total + last_y[k].astype(F32) + last_z[k].astype(F32)
    text_grad_ref[...] = total
    arrived(out_block)
    total = image_own[0:ROWS]
    for k in range(3):
        total = total + last_block[k].astype(F32)
    image_grad_ref[...] = total
    loss_ref[...] = jnp.full(loss_ref.shape, jnp.sum(take(2, gifts)) / 8192.0, F32)
    for group, whole in enumerate(groups):
        pltpu.make_async_copy(whole, whole, send.at[group]).wait()


def finish(loss_ref, image_ref, text_ref, loss_out, image_out, text_out, sems):
    copies = [
        pltpu.make_async_copy(image_ref, image_out, sems.at[0]),
        pltpu.make_async_copy(text_ref, text_out, sems.at[1]),
        pltpu.make_async_copy(loss_ref.at[pl.ds(0, 1)], loss_out, sems.at[2]),
    ]
    for made in copies:
        made.start()
    for made in copies:
        made.wait()


def local(image_embed, text_embed, logit_scale, logit_bias):
    width = image_embed.shape[1]
    vmem = pl.BlockSpec(memory_space=pltpu.VMEM)
    hbm = pl.BlockSpec(memory_space=pltpu.HBM)
    dma = pltpu.SemaphoreType.DMA
    grad = jax.ShapeDtypeStruct((ROWS, width), F32)
    loss, image_grad, text_grad = pl.pallas_call(
        kernel,
        out_shape=(jax.ShapeDtypeStruct((8, 128), F32), grad, grad),
        in_specs=[hbm, hbm, hbm, hbm],
        out_specs=(vmem, vmem, vmem),
        scratch_shapes=[
            pltpu.VMEM((2 * SET, width), BF16),
            pltpu.VMEM((2, 4, 4, ROWS, width), BF16),
            pltpu.VMEM((SET, 2 * SET), BF16),
            pltpu.VMEM((4, 4, ROWS, width), BF16),
            pltpu.VMEM((3, ROWS, CUT), F32),
            pltpu.VMEM((3, ROWS, width - CUT), F32),
            pltpu.VMEM((ROWS, width), F32),
            pltpu.VMEM((3, 3, ROWS, CUT), BF16),
            pltpu.VMEM((3, 3, ROWS, width - CUT), BF16),
            pltpu.VMEM((3, ROWS, width), BF16),
            pltpu.VMEM((3, ROWS, width), BF16),
            pltpu.VMEM((12 * ROWS, width), BF16),
            pltpu.VMEM((4 * ROWS, width), F32),
            pltpu.VMEM((3, 4 * ROWS, width), BF16),
            pltpu.VMEM((3 * ROWS, width), BF16),
            pltpu.VMEM((3, ROWS, width), BF16),
            pltpu.VMEM((3, 8, 8, 128), F32),
            pltpu.SMEM((2, 1), F32),
            dma((4,)),
            dma((19,)),
            dma((19,)),
        ],
        compiler_params=pltpu.CompilerParams(
            collective_id=0, has_side_effects=True, vmem_limit_bytes=48 * 2**20
        ),
        name="pairs",
    )(
        pltpu.with_memory_space_constraint(image_embed, pltpu.HBM),
        pltpu.with_memory_space_constraint(text_embed, pltpu.HBM),
        logit_scale,
        logit_bias,
    )
    loss, image_grad, text_grad = pl.pallas_call(
        finish,
        out_shape=(jax.ShapeDtypeStruct((1, 128), F32), grad, grad),
        in_specs=[vmem, vmem, vmem],
        out_specs=(hbm, hbm, hbm),
        scratch_shapes=[dma((3,))],
        compiler_params=pltpu.CompilerParams(vmem_limit_bytes=2**20),
        name="finish",
    )(loss, image_grad, text_grad)
    return loss[0, 0:1], image_grad, text_grad


def solution(mesh):
    rows = P(("wide", "narrow"), None)
    return jax.shard_map(
        local, mesh=mesh, in_specs=(rows, rows, P(), P()), out_specs=(P(), rows, rows), check_vma=False
    )
```

```python
import jax
import jax.numpy as jnp
from jax import lax
from jax.experimental import pallas as pl
from jax.experimental.pallas import tpu as pltpu
from jax.sharding import PartitionSpec as P

MESH = pl.DeviceIdType.MESH
F32 = jnp.float32
BF16 = jnp.bfloat16
ROWS = 16
SET = 16 * ROWS
CUT = 640
SLOT = {1: 1, 3: 2, 2: 3}
NT = (((1,), (1,)), ((), ()))


def place():
    wide = lax.axis_index("wide")
    narrow = lax.axis_index("narrow")
    y = lax.rem(lax.div(wide, 2), 8)
    z = lax.div(wide, 16) * 4 + lax.rem(narrow, 4)
    return lax.div(narrow, 4), y, z, lax.rem(wide, 2)


def device(x, y, z, core):
    return (lax.div(z, 4) * 16 + y * 2 + core, x * 4 + lax.rem(z, 4))


def turned_logits(dots, scaling, offset, diagonal):
    logits = scaling * dots + offset
    return logits if diagonal is None else jnp.where(diagonal, -logits, logits)


def pair_weights(turned, scaling, diagonal):
    small = jnp.exp(-jnp.abs(turned))
    weights = scaling * (jnp.where(turned >= 0.0, 1.0, small) / (1.0 + small))
    if diagonal is not None:
        weights = jnp.where(diagonal, -weights, weights)
    return weights.astype(BF16)


def pair_loss(turned):
    terms = jnp.maximum(turned, 0.0) + jnp.log1p(jnp.exp(-jnp.abs(turned)))
    terms = jnp.sum(terms.reshape(-1, 8, terms.shape[-1]), axis=0)
    return sum(terms[:, k : k + 128] for k in range(0, terms.shape[-1], 128))


def kernel(
    image_ref,
    text_ref,
    scale_ref,
    bias_ref,
    loss_ref,
    image_grad_ref,
    text_grad_ref,
    images,
    texts,
    weights,
    kept,
    text_parts,
    text_near,
    text_far,
    text_own,
    came_z,
    came_y,
    last_y,
    last_z,
    image_parts,
    image_own,
    came_x,
    came_last,
    block_parts,
    last_block,
    totals,
    numbers,
    load,
    send,
    recv,
    shared_loss,
    hop,
    loss_send,
    loss_recv,
):
    x, y, z, core = place()
    steps = (2, 1, 3)
    flipped_y = y + 1 - 2 * lax.rem(y, 2)
    flipped_z = z + 1 - 2 * lax.rem(z, 2)
    all_steps = (4, 3, 5, 2, 6, 1, 7)

    def along_x(k):
        return device(lax.rem(x + k, 4), y, z, core)

    def ring_y(k):
        return device(x, lax.rem(y + k, 8), z, core)

    def ring_z(k):
        return device(x, y, lax.rem(z + k, 8), core)

    def along_y(k):
        return ring_y(2 * k)

    def along_z(k):
        return ring_z(2 * k)

    def in_block(k):
        return device(x, flipped_y if k % 2 else y, flipped_z if k // 2 else z, core)

    sibling = device(x, y, z, 1 - core)

    barrier = pltpu.get_barrier_semaphore()
    for reach in (ring_y, ring_z):
        for k in all_steps:
            pl.semaphore_signal(barrier, inc=1, device_id=reach(k), device_id_type=MESH)
    for to in (along_x(2), along_x(1), along_x(3), in_block(3), sibling):
        pl.semaphore_signal(barrier, inc=1, device_id=to, device_id_type=MESH)
    loads = [
        pltpu.make_async_copy(image_ref, images.at[pl.ds(0, ROWS)], load.at[0]),
        pltpu.make_async_copy(text_ref, texts.at[0, 0, 0], load.at[1]),
        pltpu.make_async_copy(scale_ref, numbers.at[0], load.at[2]),
        pltpu.make_async_copy(bias_ref, numbers.at[1], load.at[3]),
    ]
    for made in loads:
        made.start()
    pl.semaphore_wait(barrier, 19)

    groups = []

    def start(whole, copies, group=None):
        if group is None:
            group = len(groups)
            groups.append(whole)
        for src, dst, to in copies:
            pltpu.make_async_remote_copy(
                src_ref=src,
                dst_ref=dst,
                send_sem=send.at[group],
                recv_sem=recv.at[group],
                device_id=to,
                device_id_type=MESH,
            ).start()
        return group

    def arrived(*which):
        for group in which:
            pltpu.make_async_copy(groups[group], groups[group], recv.at[group]).wait()

    width = texts.shape[-1]
    first, near, far, rest = pl.ds(0, 1), pl.ds(1, 2), pl.ds(3, 1), pl.ds(1, 3)
    head, tail = pl.ds(0, CUT), pl.ds(CUT, width - CUT)
    bundle = 4 * ROWS

    def own_text(part, reach, along_near, ways):
        def there(slots):
            return texts.at[0, first, slots, :, part] if along_near else texts.at[0, slots, first, :, part]

        def slot(k):
            at = SLOT[4 - k]
            return texts.at[0, 0, at, :, part] if along_near else texts.at[0, at, 0, :, part]

        slots = rest if len(ways) == 3 else (far if ways == (2,) else near)
        return start(there(slots), [(text_ref.at[:, part], slot(k), reach(k)) for k in ways])

    from_block = start(
        images.at[pl.ds(ROWS, 3 * ROWS)],
        [(image_ref, images.at[pl.ds(k * ROWS, ROWS)], in_block(k)) for k in (3, 1, 2)],
    )
    head_y_far = own_text(head, along_y, True, (2,))
    tail_z_far = own_text(tail, along_z, False, (2,))
    head_y = own_text(head, along_y, True, (1, 3))
    tail_z = own_text(tail, along_z, False, (1, 3))
    own_x = start(
        images.at[pl.ds(0, 3 * ROWS)],
        [(image_ref, images.at[pl.ds((4 - k) * bundle, ROWS)], along_x(k)) for k in steps],
    )
    tail_y = own_text(tail, along_y, True, steps)
    head_z = own_text(head, along_z, False, steps)

    def pass_z(slots, group=None):
        return start(
            texts.at[0, rest, rest, :, head],
            [(texts.at[0, 0, slots, :, head], texts.at[0, SLOT[4 - k], slots, :, head], along_z(k)) for k in steps],
            group,
        )

    def pass_y(slots, group=None):
        return start(
            texts.at[0, rest, rest, :, tail],
            [(texts.at[0, slots, 0, :, tail], texts.at[0, slots, SLOT[4 - k], :, tail], along_y(k)) for k in steps],
            group,
        )

    arrived(from_block)
    block = pl.ds(ROWS, 3 * ROWS)
    from_x = start(
        images.at[pl.ds(0, 9 * ROWS)],
        [
            (images.at[block], images.at[pl.ds((4 - k) * bundle + ROWS, 3 * ROWS)], along_x(k))
            for k in steps
        ],
    )
    arrived(head_y)
    passed_z = pass_z(near)
    arrived(tail_z)
    passed_y = pass_y(near)
    arrived(head_y_far)
    pass_z(far, passed_z)
    arrived(tail_z_far)
    pass_y(far, passed_y)
    for made in loads:
        made.wait()
    scaling = numbers[0, 0]
    offset = numbers[1, 0]
    arrived(own_x, from_x)
    image_share = start(
        images.at[pl.ds(SET, SET)], [(images.at[pl.ds(0, SET)], images.at[pl.ds(SET, SET)], sibling)]
    )
    arrived(tail_y, head_z, passed_z, passed_y)
    text_share = start(texts.at[1], [(texts.at[0], texts.at[1], sibling)])

    rows = lax.broadcasted_iota(jnp.int32, (SET, SET), 0)
    columns = lax.broadcasted_iota(jnp.int32, (SET, SET), 1)
    diagonal = (rows == columns) & (rows < ROWS)

    stages = ((y, ring_y, all_steps), (z, ring_z, all_steps), (x, along_x, steps))

    def across(src, dst, at):
        return pltpu.make_async_remote_copy(
            src_ref=src, dst_ref=dst, send_sem=hop.at[at], recv_sem=hop.at[at + 1], device_id=sibling, device_id_type=MESH
        )

    def ring(stage):
        slot, reach, ways = stages[stage]
        mine = totals.at[stage, slot]
        return [
            pltpu.make_async_remote_copy(
                src_ref=mine,
                dst_ref=mine,
                send_sem=loss_send.at[stage],
                recv_sem=loss_recv.at[stage],
                device_id=reach(k),
                device_id_type=MESH,
            )
            for k in ways
        ], totals.at[stage, pl.ds(0, len(ways))]

    def give(stage, value):
        totals[stage, stages[stage][0]] = value
        for made in ring(stage)[0]:
            made.start()

    def take(stage):
        whole = ring(stage)[1]
        pltpu.make_async_copy(whole, whole, loss_recv.at[stage]).wait()
        value = totals[stage, 0]
        for k in range(1, len(stages[stage][2]) + 1):
            value = value + totals[stage, k]
        return value

    def on_core_1(action):
        pl.when(core == 1)(action)

    def on_core_0(action):
        pl.when(core == 0)(action)

    def loss_start(value):
        shared_loss[0] = value
        on_core_0(across(shared_loss.at[0], shared_loss.at[1], 0).start)

    def loss_y():
        across(shared_loss.at[0], shared_loss.at[1], 0).wait_recv()
        give(0, shared_loss[0] + shared_loss[1])

    def loss_end():
        shared_loss[2] = take(2)
        across(shared_loss.at[2], shared_loss.at[3], 2).start()
        loss_ref[...] = jnp.full(loss_ref.shape, jnp.sum(shared_loss[2]) / 8192.0, F32)
        across(shared_loss.at[2], shared_loss.at[3], 2).wait_send()
        for stage in range(3):
            whole = ring(stage)[1]
            pltpu.make_async_copy(whole, whole, loss_send.at[stage]).wait()

    def loss_got():
        across(shared_loss.at[2], shared_loss.at[3], 2).wait_recv()
        loss_ref[...] = jnp.full(loss_ref.shape, jnp.sum(shared_loss[3]) / 8192.0, F32)
        across(shared_loss.at[0], shared_loss.at[1], 0).wait_send()

    def text_set(half):
        return texts[half].reshape(SET, width)

    for half in (0, 1):
        if half == 1:
            arrived(image_share)
        part = slice(half * SET, (half + 1) * SET)
        mask = diagonal if half == 0 else None
        dots = lax.dot_general(text_set(0), images[part], NT, preferred_element_type=F32)
        turned = turned_logits(dots, scaling, offset, mask)
        kept[:, part] = turned
        weights[:, part] = pair_weights(turned, scaling, mask)
    loss_start(pair_loss(kept[...]))
    grads = jnp.dot(weights[...], images[...], preferred_element_type=F32).reshape(4, 4, ROWS, -1)
    text_parts[...] = grads.astype(BF16)
    text_near[...] = grads[0, 1:4, :, 0:CUT]
    text_far[...] = grads[1:4, 0, :, CUT:]
    text_own[...] = grads[0, 0]

    def to_z(there, here):
        return start(
            came_z.at[:, there],
            [(text_parts.at[SLOT[k], here, :, head], came_z.at[SLOT[4 - k] - 1, there], along_z(k)) for k in steps],
        )

    def to_y(there, here):
        return start(
            came_y.at[:, there],
            [(text_parts.at[here, SLOT[k], :, tail], came_y.at[SLOT[4 - k] - 1, there], along_y(k)) for k in steps],
        )

    to_z_far, to_y_far = to_z(pl.ds(2, 1), far), to_y(pl.ds(2, 1), far)
    to_z_near, to_y_near = to_z(pl.ds(0, 2), near), to_y(pl.ds(0, 2), near)

    on_core_1(loss_y)

    arrived(text_share)
    for half in (0, 1):
        dots = lax.dot_general(images[0:SET], text_set(half), NT, preferred_element_type=F32)
        mask = diagonal if half == 0 else None
        turned = turned_logits(dots, scaling, offset, mask)
        weights[:, half * SET : (half + 1) * SET] = pair_weights(turned, scaling, mask)
    grads = jnp.dot(weights[...], texts[...].reshape(2 * SET, width), preferred_element_type=F32)
    image_own[...] = grads[0:bundle]
    image_parts[...] = grads[bundle:].astype(BF16)
    to_x = start(
        came_x,
        [
            (image_parts.at[pl.ds((k - 1) * bundle + ROWS, 3 * ROWS)], came_x.at[3 - k], along_x(k))
            for k in steps
        ],
    )
    on_core_1(lambda: give(1, take(0)))
    def out_y(slots, ways):
        for at in slots:
            total = text_near[at - 1]
            for k in range(3):
                total = total + came_z[k, at - 1].astype(F32)
            text_parts[0, at, :, 0:CUT] = total.astype(BF16)
        return start(
            last_y.at[pl.ds(slots[0] - 1, len(slots)), :, head],
            [(text_parts.at[0, SLOT[k], :, head], last_y.at[SLOT[4 - k] - 1, :, head], along_y(k)) for k in ways],
        )

    def out_z(slots, ways):
        for at in slots:
            total = text_far[at - 1]
            for k in range(3):
                total = total + came_y[k, at - 1].astype(F32)
            text_parts[at, 0, :, CUT:] = total.astype(BF16)
        return start(
            last_z.at[pl.ds(slots[0] - 1, len(slots)), :, tail],
            [(text_parts.at[SLOT[k], 0, :, tail], last_z.at[SLOT[4 - k] - 1, :, tail], along_z(k)) for k in ways],
        )

    arrived(to_z_far)
    outs = [out_y((3,), (2,))]
    arrived(to_y_far)
    outs.append(out_z((3,), (2,)))
    last_x = start(
        came_last,
        [(image_parts.at[pl.ds((k - 1) * bundle, ROWS)], came_last.at[3 - k], along_x(k)) for k in steps],
    )
    direct_y = start(
        last_y.at[:, :, tail],
        [(text_parts.at[0, SLOT[k], :, tail], last_y.at[SLOT[4 - k] - 1, :, tail], along_y(k)) for k in steps],
    )
    direct_z = start(
        last_z.at[:, :, head],
        [(text_parts.at[SLOT[k], 0, :, head], last_z.at[SLOT[4 - k] - 1, :, head], along_z(k)) for k in steps],
    )
    arrived(to_z_near)
    outs.append(out_y((1, 2), (1, 3)))
    arrived(to_y_near)
    outs.append(out_z((1, 2), (1, 3)))
    arrived(to_x)
    total = image_own[ROWS:]
    for k in range(3):
        total = total + came_x[k].astype(F32)
    block_parts[...] = total.astype(BF16)
    out_block = start(
        last_block,
        [
            (block_parts.at[pl.ds((k - 1) * ROWS, ROWS)], last_block.at[k - 1], in_block(k))
            for k in (3, 1, 2)
        ],
    )
    on_core_1(lambda: give(2, take(1)))
    arrived(direct_y, direct_z, *outs)
    total = text_own[...]
    for k in range(3):
        total = total + last_y[k].astype(F32) + last_z[k].astype(F32)
    text_grad_ref[...] = total
    arrived(last_x, out_block)
    total = image_own[0:ROWS]
    for k in range(3):
        total = total + came_last[k].astype(F32) + last_block[k].astype(F32)
    image_grad_ref[...] = total
    on_core_1(loss_end)
    on_core_0(loss_got)
    for group, whole in enumerate(groups):
        pltpu.make_async_copy(whole, whole, send.at[group]).wait()


def finish(loss_ref, image_ref, text_ref, loss_out, image_out, text_out, sems):
    copies = [
        pltpu.make_async_copy(image_ref, image_out, sems.at[0]),
        pltpu.make_async_copy(text_ref, text_out, sems.at[1]),
        pltpu.make_async_copy(loss_ref.at[pl.ds(0, 1)], loss_out, sems.at[2]),
    ]
    for made in copies:
        made.start()
    for made in copies:
        made.wait()


def local(image_embed, text_embed, logit_scale, logit_bias):
    width = image_embed.shape[1]
    vmem = pl.BlockSpec(memory_space=pltpu.VMEM)
    hbm = pl.BlockSpec(memory_space=pltpu.HBM)
    dma = pltpu.SemaphoreType.DMA
    grad = jax.ShapeDtypeStruct((ROWS, width), F32)
    loss, image_grad, text_grad = pl.pallas_call(
        kernel,
        out_shape=(jax.ShapeDtypeStruct((8, 128), F32), grad, grad),
        in_specs=[hbm, hbm, hbm, hbm],
        out_specs=(vmem, vmem, vmem),
        scratch_shapes=[
            pltpu.VMEM((2 * SET, width), BF16),
            pltpu.VMEM((2, 4, 4, ROWS, width), BF16),
            pltpu.VMEM((SET, 2 * SET), BF16),
            pltpu.VMEM((SET, 2 * SET), F32),
            pltpu.VMEM((4, 4, ROWS, width), BF16),
            pltpu.VMEM((3, ROWS, CUT), F32),
            pltpu.VMEM((3, ROWS, width - CUT), F32),
            pltpu.VMEM((ROWS, width), F32),
            pltpu.VMEM((3, 3, ROWS, CUT), BF16),
            pltpu.VMEM((3, 3, ROWS, width - CUT), BF16),
            pltpu.VMEM((3, ROWS, width), BF16),
            pltpu.VMEM((3, ROWS, width), BF16),
            pltpu.VMEM((12 * ROWS, width), BF16),
            pltpu.VMEM((4 * ROWS, width), F32),
            pltpu.VMEM((3, 3 * ROWS, width), BF16),
            pltpu.VMEM((3, ROWS, width), BF16),
            pltpu.VMEM((3 * ROWS, width), BF16),
            pltpu.VMEM((3, ROWS, width), BF16),
            pltpu.VMEM((3, 8, 8, 128), F32),
            pltpu.SMEM((2, 1), F32),
            dma((4,)),
            dma((26,)),
            dma((26,)),
            pltpu.VMEM((4, 8, 128), F32),
            dma((4,)),
            dma((3,)),
            dma((3,)),
        ],
        compiler_params=pltpu.CompilerParams(
            collective_id=0, has_side_effects=True, vmem_limit_bytes=48 * 2**20
        ),
        name="pairs",
    )(
        pltpu.with_memory_space_constraint(image_embed, pltpu.HBM),
        pltpu.with_memory_space_constraint(text_embed, pltpu.HBM),
        logit_scale,
        logit_bias,
    )
    loss, image_grad, text_grad = pl.pallas_call(
        finish,
        out_shape=(jax.ShapeDtypeStruct((1, 128), F32), grad, grad),
        in_specs=[vmem, vmem, vmem],
        out_specs=(hbm, hbm, hbm),
        scratch_shapes=[dma((3,))],
        compiler_params=pltpu.CompilerParams(vmem_limit_bytes=2**20),
        name="finish",
    )(loss, image_grad, text_grad)
    return loss[0, 0:1], image_grad, text_grad


def solution(mesh):
    rows = P(("wide", "narrow"), None)
    return jax.shard_map(
        local, mesh=mesh, in_specs=(rows, rows, P(), P()), out_specs=(P(), rows, rows), check_vma=False
    )
```

```python
import jax
import jax.numpy as jnp
from jax import lax
from jax.experimental import pallas as pl
from jax.experimental.pallas import tpu as pltpu
from jax.sharding import PartitionSpec as P

MESH = pl.DeviceIdType.MESH
F32 = jnp.float32
BF16 = jnp.bfloat16
ROWS = 16
SET = 16 * ROWS
CUT = 640
SLOT = {1: 1, 3: 2, 2: 3}
GROUPS = 16
SENT = (30 + 30 + 32) * ROWS
NT = (((1,), (1,)), ((), ()))


def place():
    wide = lax.axis_index("wide")
    narrow = lax.axis_index("narrow")
    y = lax.rem(lax.div(wide, 2), 8)
    z = lax.div(wide, 16) * 4 + lax.rem(narrow, 4)
    return lax.div(narrow, 4), y, z, lax.rem(wide, 2)


def device(x, y, z, core):
    return (lax.div(z, 4) * 16 + y * 2 + core, x * 4 + lax.rem(z, 4))


def turned_logits(dots, scaling, offset, diagonal):
    logits = scaling * dots + offset
    return logits if diagonal is None else jnp.where(diagonal, -logits, logits)


def pair_weights(turned, scaling, diagonal):
    small = jnp.exp(-jnp.abs(turned))
    weights = scaling * (jnp.where(turned >= 0.0, 1.0, small) / (1.0 + small))
    if diagonal is not None:
        weights = jnp.where(diagonal, -weights, weights)
    return weights.astype(BF16)


def pair_loss(turned):
    terms = jnp.maximum(turned, 0.0) + jnp.log1p(jnp.exp(-jnp.abs(turned)))
    terms = jnp.sum(terms.reshape(-1, 8, terms.shape[-1]), axis=0)
    return sum(terms[:, k : k + 128] for k in range(0, terms.shape[-1], 128))


def kernel(
    image_ref,
    text_ref,
    scale_ref,
    bias_ref,
    loss_ref,
    image_grad_ref,
    text_grad_ref,
    images,
    texts,
    weights,
    kept,
    text_parts,
    text_near,
    text_far,
    text_own,
    came_z,
    came_y,
    last_text,
    image_parts,
    image_own,
    came_x,
    block_parts,
    last_image,
    totals,
    all_sent,
    numbers,
    load,
    send,
    recv,
    shared_loss,
    hop,
    loss_send,
    loss_recv,
):
    x, y, z, core = place()
    steps = (2, 1, 3)
    flipped_y = y + 1 - 2 * lax.rem(y, 2)
    flipped_z = z + 1 - 2 * lax.rem(z, 2)
    all_steps = (4, 3, 5, 2, 6, 1, 7)

    def along_x(k):
        return device(lax.rem(x + k, 4), y, z, core)

    def ring_y(k):
        return device(x, lax.rem(y + k, 8), z, core)

    def ring_z(k):
        return device(x, y, lax.rem(z + k, 8), core)

    def along_y(k):
        return ring_y(2 * k)

    def along_z(k):
        return ring_z(2 * k)

    def in_block(k):
        return device(x, flipped_y if k % 2 else y, flipped_z if k // 2 else z, core)

    sibling = device(x, y, z, 1 - core)

    barrier = pltpu.get_barrier_semaphore()
    for reach in (ring_y, ring_z):
        for k in all_steps:
            pl.semaphore_signal(barrier, inc=1, device_id=reach(k), device_id_type=MESH)
    for to in (along_x(2), along_x(1), along_x(3), in_block(3), sibling):
        pl.semaphore_signal(barrier, inc=1, device_id=to, device_id_type=MESH)
    loads = [
        pltpu.make_async_copy(image_ref, images.at[pl.ds(0, ROWS)], load.at[0]),
        pltpu.make_async_copy(text_ref, texts.at[0, 0, 0], load.at[1]),
        pltpu.make_async_copy(scale_ref, numbers.at[0], load.at[2]),
        pltpu.make_async_copy(bias_ref, numbers.at[1], load.at[3]),
    ]
    for made in loads:
        made.start()
    pl.semaphore_wait(barrier, 19)

    groups = []

    def start(whole, copies, group=None):
        if group is None:
            group = len(groups)
            groups.append(whole)
        for src, dst, to in copies:
            pltpu.make_async_remote_copy(
                src_ref=src,
                dst_ref=dst,
                send_sem=send,
                recv_sem=recv.at[group],
                device_id=to,
                device_id_type=MESH,
            ).start()
        return group

    def arrived(*which):
        for group in which:
            pltpu.make_async_copy(groups[group], groups[group], recv.at[group]).wait()

    width = texts.shape[-1]
    first, near, far, rest = pl.ds(0, 1), pl.ds(1, 2), pl.ds(3, 1), pl.ds(1, 3)
    head, tail = pl.ds(0, CUT), pl.ds(CUT, width - CUT)
    bundle = 4 * ROWS

    def own_text(part, reach, along_near, ways, group=None):
        def there(slots):
            return texts.at[0, first, slots, :, part] if along_near else texts.at[0, slots, first, :, part]

        def slot(k):
            at = SLOT[4 - k]
            return texts.at[0, 0, at, :, part] if along_near else texts.at[0, at, 0, :, part]

        return start(
            there(far if ways == (2,) else near), [(text_ref.at[:, part], slot(k), reach(k)) for k in ways], group
        )

    from_block = start(
        images.at[pl.ds(ROWS, 3 * ROWS)],
        [(image_ref, images.at[pl.ds(k * ROWS, ROWS)], in_block(k)) for k in (3, 1, 2)],
    )
    head_y_far = own_text(head, along_y, True, (2,))
    tail_z_far = own_text(tail, along_z, False, (2,))
    head_y = own_text(head, along_y, True, (1, 3))
    tail_z = own_text(tail, along_z, False, (1, 3))
    from_x = start(
        images.at[pl.ds(bundle, 3 * bundle)],
        [(image_ref, images.at[pl.ds((4 - k) * bundle, ROWS)], along_x(k)) for k in steps],
    )
    passed = start(texts.at[0, rest], [])
    own_text(tail, along_y, True, steps, passed)
    own_text(head, along_z, False, steps, passed)

    def pass_z(slots):
        start(
            texts.at[0, rest],
            [(texts.at[0, 0, slots, :, head], texts.at[0, SLOT[4 - k], slots, :, head], along_z(k)) for k in steps],
            passed,
        )

    def pass_y(slots):
        start(
            texts.at[0, rest],
            [(texts.at[0, slots, 0, :, tail], texts.at[0, slots, SLOT[4 - k], :, tail], along_y(k)) for k in steps],
            passed,
        )

    arrived(from_block)
    block = pl.ds(ROWS, 3 * ROWS)
    start(
        images.at[block],
        [
            (images.at[block], images.at[pl.ds((4 - k) * bundle + ROWS, 3 * ROWS)], along_x(k))
            for k in steps
        ],
        from_x,
    )
    arrived(head_y)
    pass_z(near)
    arrived(tail_z)
    pass_y(near)
    arrived(head_y_far)
    pass_z(far)
    arrived(tail_z_far)
    pass_y(far)
    for made in loads:
        made.wait()
    scaling = numbers[0, 0]
    offset = numbers[1, 0]
    arrived(from_x)
    image_share = start(
        images.at[pl.ds(SET, SET)], [(images.at[pl.ds(0, SET)], images.at[pl.ds(SET, SET)], sibling)]
    )
    arrived(passed)
    text_share = start(texts.at[1], [(texts.at[0], texts.at[1], sibling)])

    rows = lax.broadcasted_iota(jnp.int32, (SET, SET), 0)
    columns = lax.broadcasted_iota(jnp.int32, (SET, SET), 1)
    diagonal = (rows == columns) & (rows < ROWS)

    stages = ((y, ring_y, all_steps), (z, ring_z, all_steps), (x, along_x, steps))

    def across(src, dst, at):
        return pltpu.make_async_remote_copy(
            src_ref=src, dst_ref=dst, send_sem=hop.at[at], recv_sem=hop.at[at + 1], device_id=sibling, device_id_type=MESH
        )

    def ring(stage):
        slot, reach, ways = stages[stage]
        mine = totals.at[stage, slot]
        return [
            pltpu.make_async_remote_copy(
                src_ref=mine,
                dst_ref=mine,
                send_sem=loss_send.at[stage],
                recv_sem=loss_recv.at[stage],
                device_id=reach(k),
                device_id_type=MESH,
            )
            for k in ways
        ], totals.at[stage, pl.ds(0, len(ways))]

    def give(stage, value):
        totals[stage, stages[stage][0]] = value
        for made in ring(stage)[0]:
            made.start()

    def take(stage):
        whole = ring(stage)[1]
        pltpu.make_async_copy(whole, whole, loss_recv.at[stage]).wait()
        value = totals[stage, 0]
        for k in range(1, len(stages[stage][2]) + 1):
            value = value + totals[stage, k]
        return value

    def on_core_1(action):
        pl.when(core == 1)(action)

    def on_core_0(action):
        pl.when(core == 0)(action)

    def loss_start(value):
        shared_loss[0] = value
        on_core_0(across(shared_loss.at[0], shared_loss.at[1], 0).start)

    def loss_y():
        across(shared_loss.at[0], shared_loss.at[1], 0).wait_recv()
        give(0, shared_loss[0] + shared_loss[1])

    def loss_end():
        shared_loss[2] = take(2)
        across(shared_loss.at[2], shared_loss.at[3], 2).start()
        loss_ref[...] = jnp.full(loss_ref.shape, jnp.sum(shared_loss[2]) / 8192.0, F32)
        across(shared_loss.at[2], shared_loss.at[3], 2).wait_send()
        for stage in range(3):
            whole = ring(stage)[1]
            pltpu.make_async_copy(whole, whole, loss_send.at[stage]).wait()

    def loss_got():
        across(shared_loss.at[2], shared_loss.at[3], 2).wait_recv()
        loss_ref[...] = jnp.full(loss_ref.shape, jnp.sum(shared_loss[3]) / 8192.0, F32)
        across(shared_loss.at[0], shared_loss.at[1], 0).wait_send()

    def text_set(half):
        return texts[half].reshape(SET, width)

    for half in (0, 1):
        if half == 1:
            arrived(image_share)
        part = slice(half * SET, (half + 1) * SET)
        mask = diagonal if half == 0 else None
        dots = lax.dot_general(text_set(0), images[part], NT, preferred_element_type=F32)
        turned = turned_logits(dots, scaling, offset, mask)
        kept[:, part] = turned
        weights[:, part] = pair_weights(turned, scaling, mask)
    loss_start(pair_loss(kept[...]))
    grads = jnp.dot(weights[...], images[...], preferred_element_type=F32).reshape(4, 4, ROWS, -1)
    text_parts[...] = grads.astype(BF16)
    text_near[...] = grads[0, 1:4, :, 0:CUT]
    text_far[...] = grads[1:4, 0, :, CUT:]
    text_own[...] = grads[0, 0]

    def to_z(there, here):
        return start(
            came_z.at[:, there],
            [(text_parts.at[SLOT[k], here, :, head], came_z.at[SLOT[4 - k] - 1, there], along_z(k)) for k in steps],
        )

    def to_y(there, here):
        return start(
            came_y.at[:, there],
            [(text_parts.at[here, SLOT[k], :, tail], came_y.at[SLOT[4 - k] - 1, there], along_y(k)) for k in steps],
        )

    to_z_far, to_y_far = to_z(pl.ds(2, 1), far), to_y(pl.ds(2, 1), far)
    to_z_near, to_y_near = to_z(pl.ds(0, 2), near), to_y(pl.ds(0, 2), near)

    on_core_1(loss_y)

    arrived(text_share)
    for half in (0, 1):
        dots = lax.dot_general(images[0:SET], text_set(half), NT, preferred_element_type=F32)
        mask = diagonal if half == 0 else None
        turned = turned_logits(dots, scaling, offset, mask)
        weights[:, half * SET : (half + 1) * SET] = pair_weights(turned, scaling, mask)
    grads = jnp.dot(weights[...], texts[...].reshape(2 * SET, width), preferred_element_type=F32)
    image_own[...] = grads[0:bundle]
    image_parts[...] = grads[bundle:].astype(BF16)
    to_x = start(
        came_x,
        [
            (image_parts.at[pl.ds((k - 1) * bundle + ROWS, 3 * ROWS)], came_x.at[3 - k], along_x(k))
            for k in steps
        ],
    )
    on_core_1(lambda: give(1, take(0)))
    def out_y(slots, ways):
        for at in slots:
            total = text_near[at - 1]
            for k in range(3):
                total = total + came_z[k, at - 1].astype(F32)
            text_parts[0, at, :, 0:CUT] = total.astype(BF16)
        start(
            last_text,
            [(text_parts.at[0, SLOT[k], :, head], last_text.at[0, SLOT[4 - k] - 1, :, head], along_y(k)) for k in ways],
            text_end,
        )

    def out_z(slots, ways):
        for at in slots:
            total = text_far[at - 1]
            for k in range(3):
                total = total + came_y[k, at - 1].astype(F32)
            text_parts[at, 0, :, CUT:] = total.astype(BF16)
        start(
            last_text,
            [(text_parts.at[SLOT[k], 0, :, tail], last_text.at[1, SLOT[4 - k] - 1, :, tail], along_z(k)) for k in ways],
            text_end,
        )

    text_end = start(last_text, [])
    image_end = start(last_image, [])
    arrived(to_z_far)
    out_y((3,), (2,))
    arrived(to_y_far)
    out_z((3,), (2,))
    start(
        last_image,
        [(image_parts.at[pl.ds((k - 1) * bundle, ROWS)], last_image.at[0, 3 - k], along_x(k)) for k in steps],
        image_end,
    )
    start(
        last_text,
        [(text_parts.at[0, SLOT[k], :, tail], last_text.at[0, SLOT[4 - k] - 1, :, tail], along_y(k)) for k in steps]
        + [(text_parts.at[SLOT[k], 0, :, head], last_text.at[1, SLOT[4 - k] - 1, :, head], along_z(k)) for k in steps],
        text_end,
    )
    arrived(to_z_near)
    out_y((1, 2), (1, 3))
    arrived(to_y_near)
    out_z((1, 2), (1, 3))
    arrived(to_x)
    total = image_own[ROWS:]
    for k in range(3):
        total = total + came_x[k].astype(F32)
    block_parts[...] = total.astype(BF16)
    start(
        last_image,
        [
            (block_parts.at[pl.ds((k - 1) * ROWS, ROWS)], last_image.at[1, k - 1], in_block(k))
            for k in (3, 1, 2)
        ],
        image_end,
    )
    on_core_1(lambda: give(2, take(1)))
    arrived(text_end)
    total = text_own[...]
    for k in range(3):
        total = total + last_text[0, k].astype(F32) + last_text[1, k].astype(F32)
    text_grad_ref[...] = total
    arrived(image_end)
    total = image_own[0:ROWS]
    for k in range(3):
        total = total + last_image[0, k].astype(F32) + last_image[1, k].astype(F32)
    image_grad_ref[...] = total
    on_core_1(loss_end)
    on_core_0(loss_got)
    pltpu.make_async_copy(all_sent, all_sent, send).wait()


def finish(loss_ref, image_ref, text_ref, loss_out, image_out, text_out, sems):
    copies = [
        pltpu.make_async_copy(image_ref, image_out, sems.at[0]),
        pltpu.make_async_copy(text_ref, text_out, sems.at[1]),
        pltpu.make_async_copy(loss_ref.at[pl.ds(0, 1)], loss_out, sems.at[2]),
    ]
    for made in copies:
        made.start()
    for made in copies:
        made.wait()


def local(image_embed, text_embed, logit_scale, logit_bias):
    width = image_embed.shape[1]
    vmem = pl.BlockSpec(memory_space=pltpu.VMEM)
    hbm = pl.BlockSpec(memory_space=pltpu.HBM)
    dma = pltpu.SemaphoreType.DMA
    grad = jax.ShapeDtypeStruct((ROWS, width), F32)
    loss, image_grad, text_grad = pl.pallas_call(
        kernel,
        out_shape=(jax.ShapeDtypeStruct((8, 128), F32), grad, grad),
        in_specs=[hbm, hbm, hbm, hbm],
        out_specs=(vmem, vmem, vmem),
        scratch_shapes=[
            pltpu.VMEM((2 * SET, width), BF16),
            pltpu.VMEM((2, 4, 4, ROWS, width), BF16),
            pltpu.VMEM((SET, 2 * SET), BF16),
            pltpu.VMEM((SET, 2 * SET), F32),
            pltpu.VMEM((4, 4, ROWS, width), BF16),
            pltpu.VMEM((3, ROWS, CUT), F32),
            pltpu.VMEM((3, ROWS, width - CUT), F32),
            pltpu.VMEM((ROWS, width), F32),
            pltpu.VMEM((3, 3, ROWS, CUT), BF16),
            pltpu.VMEM((3, 3, ROWS, width - CUT), BF16),
            pltpu.VMEM((2, 3, ROWS, width), BF16),
            pltpu.VMEM((12 * ROWS, width), BF16),
            pltpu.VMEM((4 * ROWS, width), F32),
            pltpu.VMEM((3, 3 * ROWS, width), BF16),
            pltpu.VMEM((3 * ROWS, width), BF16),
            pltpu.VMEM((2, 3, ROWS, width), BF16),
            pltpu.VMEM((3, 8, 8, 128), F32),
            pltpu.VMEM((SENT, width), BF16),
            pltpu.SMEM((2, 1), F32),
            dma((4,)),
            dma,
            dma((GROUPS,)),
            pltpu.VMEM((4, 8, 128), F32),
            dma((4,)),
            dma((3,)),
            dma((3,)),
        ],
        compiler_params=pltpu.CompilerParams(
            collective_id=0, has_side_effects=True, vmem_limit_bytes=48 * 2**20
        ),
        name="pairs",
    )(
        pltpu.with_memory_space_constraint(image_embed, pltpu.HBM),
        pltpu.with_memory_space_constraint(text_embed, pltpu.HBM),
        logit_scale,
        logit_bias,
    )
    loss, image_grad, text_grad = pl.pallas_call(
        finish,
        out_shape=(jax.ShapeDtypeStruct((1, 128), F32), grad, grad),
        in_specs=[vmem, vmem, vmem],
        out_specs=(hbm, hbm, hbm),
        scratch_shapes=[dma((3,))],
        compiler_params=pltpu.CompilerParams(vmem_limit_bytes=2**20),
        name="finish",
    )(loss, image_grad, text_grad)
    return loss[0, 0:1], image_grad, text_grad


def solution(mesh):
    rows = P(("wide", "narrow"), None)
    return jax.shard_map(
        local, mesh=mesh, in_specs=(rows, rows, P(), P()), out_specs=(P(), rows, rows), check_vma=False
    )
```

```python
import jax
import jax.numpy as jnp
from jax import lax
from jax.experimental import pallas as pl
from jax.experimental.pallas import tpu as pltpu
from jax.sharding import PartitionSpec as P

MESH = pl.DeviceIdType.MESH
F32 = jnp.float32
BF16 = jnp.bfloat16
ROWS = 16
SET = 16 * ROWS
CUT = 640
SLOT = {1: 1, 3: 2, 2: 3}
GROUPS = 16
SENT = (30 + 30 + 32) * ROWS
NT = (((1,), (1,)), ((), ()))


def place():
    wide = lax.axis_index("wide")
    narrow = lax.axis_index("narrow")
    y = lax.rem(lax.div(wide, 2), 8)
    z = lax.div(wide, 16) * 4 + lax.rem(narrow, 4)
    return lax.div(narrow, 4), y, z, lax.rem(wide, 2)


def device(x, y, z, core):
    return (lax.div(z, 4) * 16 + y * 2 + core, x * 4 + lax.rem(z, 4))


def turned_logits(dots, scaling, offset, diagonal):
    logits = scaling * dots + offset
    return logits if diagonal is None else jnp.where(diagonal, -logits, logits)


def pair_weights(turned, scaling, diagonal):
    small = jnp.exp(-jnp.abs(turned))
    weights = scaling * (jnp.where(turned >= 0.0, 1.0, small) / (1.0 + small))
    if diagonal is not None:
        weights = jnp.where(diagonal, -weights, weights)
    return weights.astype(BF16)


def pair_loss(turned):
    terms = jnp.maximum(turned, 0.0) + jnp.log1p(jnp.exp(-jnp.abs(turned)))
    terms = jnp.sum(terms.reshape(-1, 8, terms.shape[-1]), axis=0)
    return sum(terms[:, k : k + 128] for k in range(0, terms.shape[-1], 128))


def kernel(
    image_ref,
    text_ref,
    scale_ref,
    bias_ref,
    loss_ref,
    image_grad_ref,
    text_grad_ref,
    images,
    texts,
    weights,
    kept,
    text_parts,
    text_near,
    text_far,
    text_own,
    came_z,
    came_y,
    last_text,
    image_parts,
    image_own,
    came_x,
    block_parts,
    last_image,
    totals,
    all_sent,
    numbers,
    load,
    send,
    recv,
    shared_loss,
    hop,
    loss_send,
    loss_recv,
):
    x, y, z, core = place()
    steps = (2, 1, 3)
    flipped_y = y + 1 - 2 * lax.rem(y, 2)
    flipped_z = z + 1 - 2 * lax.rem(z, 2)
    all_steps = (4, 3, 5, 2, 6, 1, 7)

    def along_x(k):
        return device(lax.rem(x + k, 4), y, z, core)

    def ring_y(k):
        return device(x, lax.rem(y + k, 8), z, core)

    def ring_z(k):
        return device(x, y, lax.rem(z + k, 8), core)

    def along_y(k):
        return ring_y(2 * k)

    def along_z(k):
        return ring_z(2 * k)

    def in_block(k):
        return device(x, flipped_y if k % 2 else y, flipped_z if k // 2 else z, core)

    sibling = device(x, y, z, 1 - core)

    barrier = pltpu.get_barrier_semaphore()
    for reach in (ring_y, ring_z):
        for k in all_steps:
            pl.semaphore_signal(barrier, inc=1, device_id=reach(k), device_id_type=MESH)
    for to in (along_x(2), along_x(1), along_x(3), in_block(3), sibling):
        pl.semaphore_signal(barrier, inc=1, device_id=to, device_id_type=MESH)
    loads = [
        pltpu.make_async_copy(image_ref, images.at[pl.ds(0, ROWS)], load.at[0]),
        pltpu.make_async_copy(text_ref, texts.at[0, 0, 0], load.at[1]),
        pltpu.make_async_copy(scale_ref, numbers.at[0], load.at[2]),
        pltpu.make_async_copy(bias_ref, numbers.at[1], load.at[3]),
    ]
    for made in loads:
        made.start()
    pl.semaphore_wait(barrier, 19)

    groups = []

    def start(whole, copies, group=None):
        if group is None:
            group = len(groups)
            groups.append(whole)
        for src, dst, to in copies:
            pltpu.make_async_remote_copy(
                src_ref=src,
                dst_ref=dst,
                send_sem=send,
                recv_sem=recv.at[group],
                device_id=to,
                device_id_type=MESH,
            ).start()
        return group

    def arrived(*which):
        for group in which:
            pltpu.make_async_copy(groups[group], groups[group], recv.at[group]).wait()

    width = texts.shape[-1]
    first, near, far, rest = pl.ds(0, 1), pl.ds(1, 2), pl.ds(3, 1), pl.ds(1, 3)
    head, tail = pl.ds(0, CUT), pl.ds(CUT, width - CUT)
    bundle = 4 * ROWS

    def own_text(part, reach, along_near, ways, group=None):
        def there(slots):
            return texts.at[0, first, slots, :, part] if along_near else texts.at[0, slots, first, :, part]

        def slot(k):
            at = SLOT[4 - k]
            return texts.at[0, 0, at, :, part] if along_near else texts.at[0, at, 0, :, part]

        return start(
            there(far if ways == (2,) else near), [(text_ref.at[:, part], slot(k), reach(k)) for k in ways], group
        )

    from_block = start(
        images.at[pl.ds(ROWS, 3 * ROWS)],
        [(image_ref, images.at[pl.ds(k * ROWS, ROWS)], in_block(k)) for k in (3, 1, 2)],
    )
    head_y_far = own_text(head, along_y, True, (2,))
    tail_z_far = own_text(tail, along_z, False, (2,))
    head_y = own_text(head, along_y, True, (1, 3))
    tail_z = own_text(tail, along_z, False, (1, 3))
    from_x = start(
        images.at[pl.ds(bundle, 3 * bundle)],
        [(image_ref, images.at[pl.ds((4 - k) * bundle, ROWS)], along_x(k)) for k in steps],
    )
    passed = start(texts.at[0, rest], [])
    own_text(tail, along_y, True, steps, passed)
    own_text(head, along_z, False, steps, passed)

    def pass_z(slots):
        start(
            texts.at[0, rest],
            [(texts.at[0, 0, slots, :, head], texts.at[0, SLOT[4 - k], slots, :, head], along_z(k)) for k in steps],
            passed,
        )

    def pass_y(slots):
        start(
            texts.at[0, rest],
            [(texts.at[0, slots, 0, :, tail], texts.at[0, slots, SLOT[4 - k], :, tail], along_y(k)) for k in steps],
            passed,
        )

    arrived(from_block)
    block = pl.ds(ROWS, 3 * ROWS)
    start(
        images.at[block],
        [
            (images.at[block], images.at[pl.ds((4 - k) * bundle + ROWS, 3 * ROWS)], along_x(k))
            for k in steps
        ],
        from_x,
    )
    arrived(head_y)
    pass_z(near)
    arrived(tail_z)
    pass_y(near)
    arrived(head_y_far)
    pass_z(far)
    arrived(tail_z_far)
    pass_y(far)
    for made in loads:
        made.wait()
    scaling = numbers[0, 0]
    offset = numbers[1, 0]
    arrived(from_x)
    image_share = start(
        images.at[pl.ds(SET, SET)], [(images.at[pl.ds(0, SET)], images.at[pl.ds(SET, SET)], sibling)]
    )
    arrived(passed)
    text_share = start(texts.at[1], [(texts.at[0], texts.at[1], sibling)])

    rows = lax.broadcasted_iota(jnp.int32, (SET, SET), 0)
    columns = lax.broadcasted_iota(jnp.int32, (SET, SET), 1)
    diagonal = (rows == columns) & (rows < ROWS)

    stages = ((y, ring_y, all_steps), (z, ring_z, all_steps), (x, along_x, steps))

    def across(src, dst, at):
        return pltpu.make_async_remote_copy(
            src_ref=src, dst_ref=dst, send_sem=hop.at[at], recv_sem=hop.at[at + 1], device_id=sibling, device_id_type=MESH
        )

    def ring(stage):
        slot, reach, ways = stages[stage]
        mine = totals.at[stage, slot]
        return [
            pltpu.make_async_remote_copy(
                src_ref=mine,
                dst_ref=mine,
                send_sem=loss_send.at[stage],
                recv_sem=loss_recv.at[stage],
                device_id=reach(k),
                device_id_type=MESH,
            )
            for k in ways
        ], totals.at[stage, pl.ds(0, len(ways))]

    def give(stage, value):
        totals[stage, stages[stage][0]] = value
        for made in ring(stage)[0]:
            made.start()

    def take(stage):
        whole = ring(stage)[1]
        pltpu.make_async_copy(whole, whole, loss_recv.at[stage]).wait()
        value = totals[stage, 0]
        for k in range(1, len(stages[stage][2]) + 1):
            value = value + totals[stage, k]
        return value

    def on_core_1(action):
        pl.when(core == 1)(action)

    def on_core_0(action):
        pl.when(core == 0)(action)

    def loss_start(value):
        shared_loss[0] = value
        on_core_0(across(shared_loss.at[0], shared_loss.at[1], 0).start)

    def loss_y():
        across(shared_loss.at[0], shared_loss.at[1], 0).wait_recv()
        give(0, shared_loss[0] + shared_loss[1])

    def loss_end():
        shared_loss[2] = take(2)
        across(shared_loss.at[2], shared_loss.at[3], 2).start()
        loss_ref[...] = jnp.full(loss_ref.shape, jnp.sum(shared_loss[2]) / 8192.0, F32)
        across(shared_loss.at[2], shared_loss.at[3], 2).wait_send()
        for stage in range(3):
            whole = ring(stage)[1]
            pltpu.make_async_copy(whole, whole, loss_send.at[stage]).wait()

    def loss_got():
        across(shared_loss.at[2], shared_loss.at[3], 2).wait_recv()
        loss_ref[...] = jnp.full(loss_ref.shape, jnp.sum(shared_loss[3]) / 8192.0, F32)
        across(shared_loss.at[0], shared_loss.at[1], 0).wait_send()

    def text_set(half):
        return texts[half].reshape(SET, width)

    arrived(image_share)
    for half in (0, 1):
        part = slice(half * SET, (half + 1) * SET)
        mask = diagonal if half == 0 else None
        dots = lax.dot_general(text_set(0), images[part], NT, preferred_element_type=F32)
        turned = turned_logits(dots, scaling, offset, mask)
        kept[:, part] = turned
        weights[:, part] = pair_weights(turned, scaling, mask)
    loss_start(pair_loss(kept[...]))
    grads = jnp.dot(weights[...], images[...], preferred_element_type=F32).reshape(4, 4, ROWS, -1)
    text_parts[...] = grads.astype(BF16)
    text_near[...] = grads[0, 1:4, :, 0:CUT]
    text_far[...] = grads[1:4, 0, :, CUT:]
    text_own[...] = grads[0, 0]

    def to_z(there, here):
        return start(
            came_z.at[:, there],
            [(text_parts.at[SLOT[k], here, :, head], came_z.at[SLOT[4 - k] - 1, there], along_z(k)) for k in steps],
        )

    def to_y(there, here):
        return start(
            came_y.at[:, there],
            [(text_parts.at[here, SLOT[k], :, tail], came_y.at[SLOT[4 - k] - 1, there], along_y(k)) for k in steps],
        )

    to_z_far, to_y_far = to_z(pl.ds(2, 1), far), to_y(pl.ds(2, 1), far)
    to_z_near, to_y_near = to_z(pl.ds(0, 2), near), to_y(pl.ds(0, 2), near)

    on_core_1(loss_y)

    arrived(text_share)
    for half in (0, 1):
        dots = lax.dot_general(images[0:SET], text_set(half), NT, preferred_element_type=F32)
        mask = diagonal if half == 0 else None
        turned = turned_logits(dots, scaling, offset, mask)
        weights[:, half * SET : (half + 1) * SET] = pair_weights(turned, scaling, mask)
    grads = jnp.dot(weights[...], texts[...].reshape(2 * SET, width), preferred_element_type=F32)
    image_own[...] = grads[0:bundle]
    image_parts[...] = grads[bundle:].astype(BF16)
    to_x = start(
        came_x,
        [
            (image_parts.at[pl.ds((k - 1) * bundle + ROWS, 3 * ROWS)], came_x.at[3 - k], along_x(k))
            for k in steps
        ],
    )
    on_core_1(lambda: give(1, take(0)))
    def out_y(slots, ways):
        for at in slots:
            total = text_near[at - 1]
            for k in range(3):
                total = total + came_z[k, at - 1].astype(F32)
            text_parts[0, at, :, 0:CUT] = total.astype(BF16)
        start(
            last_text,
            [(text_parts.at[0, SLOT[k], :, head], last_text.at[0, SLOT[4 - k] - 1, :, head], along_y(k)) for k in ways],
            text_end,
        )

    def out_z(slots, ways):
        for at in slots:
            total = text_far[at - 1]
            for k in range(3):
                total = total + came_y[k, at - 1].astype(F32)
            text_parts[at, 0, :, CUT:] = total.astype(BF16)
        start(
            last_text,
            [(text_parts.at[SLOT[k], 0, :, tail], last_text.at[1, SLOT[4 - k] - 1, :, tail], along_z(k)) for k in ways],
            text_end,
        )

    text_end = start(last_text, [])
    image_end = start(last_image, [])
    arrived(to_z_far)
    out_y((3,), (2,))
    arrived(to_y_far)
    out_z((3,), (2,))
    start(
        last_image,
        [(image_parts.at[pl.ds((k - 1) * bundle, ROWS)], last_image.at[0, 3 - k], along_x(k)) for k in steps],
        image_end,
    )
    start(
        last_text,
        [(text_parts.at[0, SLOT[k], :, tail], last_text.at[0, SLOT[4 - k] - 1, :, tail], along_y(k)) for k in steps]
        + [(text_parts.at[SLOT[k], 0, :, head], last_text.at[1, SLOT[4 - k] - 1, :, head], along_z(k)) for k in steps],
        text_end,
    )
    arrived(to_z_near)
    out_y((1, 2), (1, 3))
    arrived(to_y_near)
    out_z((1, 2), (1, 3))
    arrived(to_x)
    total = image_own[ROWS:]
    for k in range(3):
        total = total + came_x[k].astype(F32)
    block_parts[...] = total.astype(BF16)
    start(
        last_image,
        [
            (block_parts.at[pl.ds((k - 1) * ROWS, ROWS)], last_image.at[1, k - 1], in_block(k))
            for k in (3, 1, 2)
        ],
        image_end,
    )
    on_core_1(lambda: give(2, take(1)))
    arrived(text_end)
    total = text_own[...]
    for k in range(3):
        total = total + last_text[0, k].astype(F32) + last_text[1, k].astype(F32)
    text_grad_ref[...] = total
    arrived(image_end)
    total = image_own[0:ROWS]
    for k in range(3):
        total = total + last_image[0, k].astype(F32) + last_image[1, k].astype(F32)
    image_grad_ref[...] = total
    on_core_1(loss_end)
    on_core_0(loss_got)
    pltpu.make_async_copy(all_sent, all_sent, send).wait()


def finish(loss_ref, image_ref, text_ref, loss_out, image_out, text_out, sems):
    copies = [
        pltpu.make_async_copy(image_ref, image_out, sems.at[0]),
        pltpu.make_async_copy(text_ref, text_out, sems.at[1]),
        pltpu.make_async_copy(loss_ref.at[pl.ds(0, 1)], loss_out, sems.at[2]),
    ]
    for made in copies:
        made.start()
    for made in copies:
        made.wait()


def local(image_embed, text_embed, logit_scale, logit_bias):
    width = image_embed.shape[1]
    vmem = pl.BlockSpec(memory_space=pltpu.VMEM)
    hbm = pl.BlockSpec(memory_space=pltpu.HBM)
    dma = pltpu.SemaphoreType.DMA
    grad = jax.ShapeDtypeStruct((ROWS, width), F32)
    loss, image_grad, text_grad = pl.pallas_call(
        kernel,
        out_shape=(jax.ShapeDtypeStruct((8, 128), F32), grad, grad),
        in_specs=[hbm, hbm, hbm, hbm],
        out_specs=(vmem, vmem, vmem),
        scratch_shapes=[
            pltpu.VMEM((2 * SET, width), BF16),
            pltpu.VMEM((2, 4, 4, ROWS, width), BF16),
            pltpu.VMEM((SET, 2 * SET), BF16),
            pltpu.VMEM((SET, 2 * SET), F32),
            pltpu.VMEM((4, 4, ROWS, width), BF16),
            pltpu.VMEM((3, ROWS, CUT), F32),
            pltpu.VMEM((3, ROWS, width - CUT), F32),
            pltpu.VMEM((ROWS, width), F32),
            pltpu.VMEM((3, 3, ROWS, CUT), BF16),
            pltpu.VMEM((3, 3, ROWS, width - CUT), BF16),
            pltpu.VMEM((2, 3, ROWS, width), BF16),
            pltpu.VMEM((12 * ROWS, width), BF16),
            pltpu.VMEM((4 * ROWS, width), F32),
            pltpu.VMEM((3, 3 * ROWS, width), BF16),
            pltpu.VMEM((3 * ROWS, width), BF16),
            pltpu.VMEM((2, 3, ROWS, width), BF16),
            pltpu.VMEM((3, 8, 8, 128), F32),
            pltpu.VMEM((SENT, width), BF16),
            pltpu.SMEM((2, 1), F32),
            dma((4,)),
            dma,
            dma((GROUPS,)),
            pltpu.VMEM((4, 8, 128), F32),
            dma((4,)),
            dma((3,)),
            dma((3,)),
        ],
        compiler_params=pltpu.CompilerParams(
            collective_id=0, has_side_effects=True, vmem_limit_bytes=48 * 2**20
        ),
        name="pairs",
    )(
        pltpu.with_memory_space_constraint(image_embed, pltpu.HBM),
        pltpu.with_memory_space_constraint(text_embed, pltpu.HBM),
        logit_scale,
        logit_bias,
    )
    loss, image_grad, text_grad = pl.pallas_call(
        finish,
        out_shape=(jax.ShapeDtypeStruct((1, 128), F32), grad, grad),
        in_specs=[vmem, vmem, vmem],
        out_specs=(hbm, hbm, hbm),
        scratch_shapes=[dma((3,))],
        compiler_params=pltpu.CompilerParams(vmem_limit_bytes=2**20),
        name="finish",
    )(loss, image_grad, text_grad)
    return loss[0, 0:1], image_grad, text_grad


def solution(mesh):
    rows = P(("wide", "narrow"), None)
    return jax.shard_map(
        local, mesh=mesh, in_specs=(rows, rows, P(), P()), out_specs=(P(), rows, rows), check_vma=False
    )
```

```python
import jax
import jax.numpy as jnp
from jax import lax
from jax.experimental import pallas as pl
from jax.experimental.pallas import tpu as pltpu
from jax.sharding import PartitionSpec as P

MESH = pl.DeviceIdType.MESH
F32 = jnp.float32
BF16 = jnp.bfloat16
ROWS = 16
SET = 16 * ROWS
CUT = 640
SLOT = {1: 1, 3: 2, 2: 3}
GROUPS = 16
SENT = (30 + 30 + 32) * ROWS
NT = (((1,), (1,)), ((), ()))


def place():
    wide = lax.axis_index("wide")
    narrow = lax.axis_index("narrow")
    y = lax.rem(lax.div(wide, 2), 8)
    z = lax.div(wide, 16) * 4 + lax.rem(narrow, 4)
    return lax.div(narrow, 4), y, z, lax.rem(wide, 2)


def device(x, y, z, core):
    return (lax.div(z, 4) * 16 + y * 2 + core, x * 4 + lax.rem(z, 4))


def turned_logits(dots, scaling, offset, diagonal):
    logits = scaling * dots + offset
    return logits if diagonal is None else jnp.where(diagonal, -logits, logits)


def pair_weights(turned, scaling, diagonal):
    small = jnp.exp(-jnp.abs(turned))
    weights = scaling * (jnp.where(turned >= 0.0, 1.0, small) / (1.0 + small))
    if diagonal is not None:
        weights = jnp.where(diagonal, -weights, weights)
    return weights.astype(BF16)


def pair_loss(turned):
    terms = jnp.maximum(turned, 0.0) + jnp.log1p(jnp.exp(-jnp.abs(turned)))
    terms = jnp.sum(terms.reshape(-1, 8, terms.shape[-1]), axis=0)
    return sum(terms[:, k : k + 128] for k in range(0, terms.shape[-1], 128))


def kernel(
    image_ref,
    text_ref,
    scale_ref,
    bias_ref,
    loss_ref,
    image_grad_ref,
    text_grad_ref,
    images,
    texts,
    weights,
    kept,
    text_parts,
    text_near,
    text_far,
    text_own,
    came_z,
    came_y,
    last_text,
    image_parts,
    image_own,
    came_x,
    block_parts,
    last_image,
    totals,
    all_sent,
    numbers,
    load,
    send,
    recv,
    shared_loss,
    hop,
    loss_send,
    loss_recv,
):
    x, y, z, core = place()
    steps = (2, 1, 3)
    flipped_y = y + 1 - 2 * lax.rem(y, 2)
    flipped_z = z + 1 - 2 * lax.rem(z, 2)
    all_steps = (4, 3, 5, 2, 6, 1, 7)

    def along_x(k):
        return device(lax.rem(x + k, 4), y, z, core)

    def ring_y(k):
        return device(x, lax.rem(y + k, 8), z, core)

    def ring_z(k):
        return device(x, y, lax.rem(z + k, 8), core)

    def along_y(k):
        return ring_y(2 * k)

    def along_z(k):
        return ring_z(2 * k)

    def in_block(k):
        return device(x, flipped_y if k % 2 else y, flipped_z if k // 2 else z, core)

    sibling = device(x, y, z, 1 - core)

    barrier = pltpu.get_barrier_semaphore()
    for reach in (along_y, along_z, along_x, in_block):
        for k in steps:
            pl.semaphore_signal(barrier, inc=1, device_id=reach(k), device_id_type=MESH)
    pl.semaphore_signal(barrier, inc=1, device_id=sibling, device_id_type=MESH)
    loads = [
        pltpu.make_async_copy(image_ref, images.at[pl.ds(0, ROWS)], load.at[0]),
        pltpu.make_async_copy(text_ref, texts.at[0, 0, 0], load.at[1]),
        pltpu.make_async_copy(scale_ref, numbers.at[0], load.at[2]),
        pltpu.make_async_copy(bias_ref, numbers.at[1], load.at[3]),
    ]
    for made in loads:
        made.start()
    pl.semaphore_wait(barrier, 13)

    groups = []

    def start(whole, copies, group=None):
        if group is None:
            group = len(groups)
            groups.append(whole)
        for src, dst, to in copies:
            pltpu.make_async_remote_copy(
                src_ref=src,
                dst_ref=dst,
                send_sem=send,
                recv_sem=recv.at[group],
                device_id=to,
                device_id_type=MESH,
            ).start()
        return group

    def arrived(*which):
        for group in which:
            pltpu.make_async_copy(groups[group], groups[group], recv.at[group]).wait()

    width = texts.shape[-1]
    first, near, far, rest = pl.ds(0, 1), pl.ds(1, 2), pl.ds(3, 1), pl.ds(1, 3)
    head, tail = pl.ds(0, CUT), pl.ds(CUT, width - CUT)
    bundle = 4 * ROWS

    def own_text(part, reach, along_near, ways, group=None):
        def there(slots):
            return texts.at[0, first, slots, :, part] if along_near else texts.at[0, slots, first, :, part]

        def slot(k):
            at = SLOT[4 - k]
            return texts.at[0, 0, at, :, part] if along_near else texts.at[0, at, 0, :, part]

        return start(
            there(far if ways == (2,) else near), [(text_ref.at[:, part], slot(k), reach(k)) for k in ways], group
        )

    from_block = start(
        images.at[pl.ds(ROWS, 3 * ROWS)],
        [(image_ref, images.at[pl.ds(k * ROWS, ROWS)], in_block(k)) for k in (3, 1, 2)],
    )
    head_y_far = own_text(head, along_y, True, (2,))
    tail_z_far = own_text(tail, along_z, False, (2,))
    head_y = own_text(head, along_y, True, (1, 3))
    tail_z = own_text(tail, along_z, False, (1, 3))
    from_x = start(
        images.at[pl.ds(bundle, 3 * bundle)],
        [(image_ref, images.at[pl.ds((4 - k) * bundle, ROWS)], along_x(k)) for k in steps],
    )
    passed = start(texts.at[0, rest], [])
    own_text(tail, along_y, True, steps, passed)
    own_text(head, along_z, False, steps, passed)

    def pass_z(slots):
        start(
            texts.at[0, rest],
            [(texts.at[0, 0, slots, :, head], texts.at[0, SLOT[4 - k], slots, :, head], along_z(k)) for k in steps],
            passed,
        )

    def pass_y(slots):
        start(
            texts.at[0, rest],
            [(texts.at[0, slots, 0, :, tail], texts.at[0, slots, SLOT[4 - k], :, tail], along_y(k)) for k in steps],
            passed,
        )

    arrived(from_block)
    block = pl.ds(ROWS, 3 * ROWS)
    start(
        images.at[block],
        [
            (images.at[block], images.at[pl.ds((4 - k) * bundle + ROWS, 3 * ROWS)], along_x(k))
            for k in steps
        ],
        from_x,
    )
    arrived(head_y)
    pass_z(near)
    arrived(tail_z)
    pass_y(near)
    arrived(head_y_far)
    pass_z(far)
    arrived(tail_z_far)
    pass_y(far)
    for made in loads:
        made.wait()
    scaling = numbers[0, 0]
    offset = numbers[1, 0]
    arrived(from_x)
    image_share = start(
        images.at[pl.ds(SET, SET)], [(images.at[pl.ds(0, SET)], images.at[pl.ds(SET, SET)], sibling)]
    )
    arrived(passed)
    text_share = start(texts.at[1], [(texts.at[0], texts.at[1], sibling)])

    rows = lax.broadcasted_iota(jnp.int32, (SET, SET), 0)
    columns = lax.broadcasted_iota(jnp.int32, (SET, SET), 1)
    diagonal = (rows == columns) & (rows < ROWS)

    stages = ((y, ring_y, all_steps), (z, ring_z, all_steps), (x, along_x, steps))

    def across(src, dst, at):
        return pltpu.make_async_remote_copy(
            src_ref=src, dst_ref=dst, send_sem=hop.at[at], recv_sem=hop.at[at + 1], device_id=sibling, device_id_type=MESH
        )

    def ring(stage):
        slot, reach, ways = stages[stage]
        mine = totals.at[stage, slot]
        return [
            pltpu.make_async_remote_copy(
                src_ref=mine,
                dst_ref=mine,
                send_sem=loss_send.at[stage],
                recv_sem=loss_recv.at[stage],
                device_id=reach(k),
                device_id_type=MESH,
            )
            for k in ways
        ], totals.at[stage, pl.ds(0, len(ways))]

    def give(stage, value):
        totals[stage, stages[stage][0]] = value
        for made in ring(stage)[0]:
            made.start()

    def take(stage):
        whole = ring(stage)[1]
        pltpu.make_async_copy(whole, whole, loss_recv.at[stage]).wait()
        value = totals[stage, 0]
        for k in range(1, len(stages[stage][2]) + 1):
            value = value + totals[stage, k]
        return value

    def on_core_1(action):
        pl.when(core == 1)(action)

    def on_core_0(action):
        pl.when(core == 0)(action)

    def loss_start(value):
        shared_loss[0] = value
        on_core_0(across(shared_loss.at[0], shared_loss.at[1], 0).start)

    def loss_y():
        across(shared_loss.at[0], shared_loss.at[1], 0).wait_recv()
        give(0, shared_loss[0] + shared_loss[1])

    def loss_end():
        shared_loss[2] = take(2)
        across(shared_loss.at[2], shared_loss.at[3], 2).start()
        loss_ref[...] = jnp.full(loss_ref.shape, jnp.sum(shared_loss[2]) / 8192.0, F32)
        across(shared_loss.at[2], shared_loss.at[3], 2).wait_send()
        for stage in range(3):
            whole = ring(stage)[1]
            pltpu.make_async_copy(whole, whole, loss_send.at[stage]).wait()

    def loss_got():
        across(shared_loss.at[2], shared_loss.at[3], 2).wait_recv()
        loss_ref[...] = jnp.full(loss_ref.shape, jnp.sum(shared_loss[3]) / 8192.0, F32)
        across(shared_loss.at[0], shared_loss.at[1], 0).wait_send()

    def text_set(half):
        return texts[half].reshape(SET, width)

    arrived(image_share)
    for half in (0, 1):
        part = slice(half * SET, (half + 1) * SET)
        mask = diagonal if half == 0 else None
        dots = lax.dot_general(text_set(0), images[part], NT, preferred_element_type=F32)
        turned = turned_logits(dots, scaling, offset, mask)
        kept[:, part] = turned
        weights[:, part] = pair_weights(turned, scaling, mask)
    loss_start(pair_loss(kept[...]))
    grads = jnp.dot(weights[...], images[...], preferred_element_type=F32).reshape(4, 4, ROWS, -1)
    text_parts[...] = grads.astype(BF16)
    text_near[...] = grads[0, 1:4, :, 0:CUT]
    text_far[...] = grads[1:4, 0, :, CUT:]
    text_own[...] = grads[0, 0]

    def to_z(there, here):
        return start(
            came_z.at[:, there],
            [(text_parts.at[SLOT[k], here, :, head], came_z.at[SLOT[4 - k] - 1, there], along_z(k)) for k in steps],
        )

    def to_y(there, here):
        return start(
            came_y.at[:, there],
            [(text_parts.at[here, SLOT[k], :, tail], came_y.at[SLOT[4 - k] - 1, there], along_y(k)) for k in steps],
        )

    to_z_far, to_y_far = to_z(pl.ds(2, 1), far), to_y(pl.ds(2, 1), far)
    to_z_near, to_y_near = to_z(pl.ds(0, 2), near), to_y(pl.ds(0, 2), near)

    on_core_1(loss_y)

    arrived(text_share)
    for half in (0, 1):
        dots = lax.dot_general(images[0:SET], text_set(half), NT, preferred_element_type=F32)
        mask = diagonal if half == 0 else None
        turned = turned_logits(dots, scaling, offset, mask)
        weights[:, half * SET : (half + 1) * SET] = pair_weights(turned, scaling, mask)
    grads = jnp.dot(weights[...], texts[...].reshape(2 * SET, width), preferred_element_type=F32)
    image_own[...] = grads[0:bundle]
    image_parts[...] = grads[bundle:].astype(BF16)
    to_x = start(
        came_x,
        [
            (image_parts.at[pl.ds((k - 1) * bundle + ROWS, 3 * ROWS)], came_x.at[3 - k], along_x(k))
            for k in steps
        ],
    )
    on_core_1(lambda: give(1, take(0)))
    def out_y(slots, ways):
        for at in slots:
            total = text_near[at - 1]
            for k in range(3):
                total = total + came_z[k, at - 1].astype(F32)
            text_parts[0, at, :, 0:CUT] = total.astype(BF16)
        start(
            last_text,
            [(text_parts.at[0, SLOT[k], :, head], last_text.at[0, SLOT[4 - k] - 1, :, head], along_y(k)) for k in ways],
            text_end,
        )

    def out_z(slots, ways):
        for at in slots:
            total = text_far[at - 1]
            for k in range(3):
                total = total + came_y[k, at - 1].astype(F32)
            text_parts[at, 0, :, CUT:] = total.astype(BF16)
        start(
            last_text,
            [(text_parts.at[SLOT[k], 0, :, tail], last_text.at[1, SLOT[4 - k] - 1, :, tail], along_z(k)) for k in ways],
            text_end,
        )

    text_end = start(last_text, [])
    image_end = start(last_image, [])
    arrived(to_z_far)
    out_y((3,), (2,))
    arrived(to_y_far)
    out_z((3,), (2,))
    start(
        last_image,
        [(image_parts.at[pl.ds((k - 1) * bundle, ROWS)], last_image.at[0, 3 - k], along_x(k)) for k in steps],
        image_end,
    )
    start(
        last_text,
        [(text_parts.at[0, SLOT[k], :, tail], last_text.at[0, SLOT[4 - k] - 1, :, tail], along_y(k)) for k in steps]
        + [(text_parts.at[SLOT[k], 0, :, head], last_text.at[1, SLOT[4 - k] - 1, :, head], along_z(k)) for k in steps],
        text_end,
    )
    arrived(to_z_near)
    out_y((1, 2), (1, 3))
    arrived(to_y_near)
    out_z((1, 2), (1, 3))
    arrived(to_x)
    total = image_own[ROWS:]
    for k in range(3):
        total = total + came_x[k].astype(F32)
    block_parts[...] = total.astype(BF16)
    start(
        last_image,
        [
            (block_parts.at[pl.ds((k - 1) * ROWS, ROWS)], last_image.at[1, k - 1], in_block(k))
            for k in (3, 1, 2)
        ],
        image_end,
    )
    on_core_1(lambda: give(2, take(1)))
    arrived(text_end)
    total = text_own[...]
    for k in range(3):
        total = total + last_text[0, k].astype(F32) + last_text[1, k].astype(F32)
    text_grad_ref[...] = total
    arrived(image_end)
    total = image_own[0:ROWS]
    for k in range(3):
        total = total + last_image[0, k].astype(F32) + last_image[1, k].astype(F32)
    image_grad_ref[...] = total
    on_core_1(loss_end)
    on_core_0(loss_got)
    pltpu.make_async_copy(all_sent, all_sent, send).wait()


def finish(loss_ref, image_ref, text_ref, loss_out, image_out, text_out, sems):
    copies = [
        pltpu.make_async_copy(image_ref, image_out, sems.at[0]),
        pltpu.make_async_copy(text_ref, text_out, sems.at[1]),
        pltpu.make_async_copy(loss_ref.at[pl.ds(0, 1)], loss_out, sems.at[2]),
    ]
    for made in copies:
        made.start()
    for made in copies:
        made.wait()


def local(image_embed, text_embed, logit_scale, logit_bias):
    width = image_embed.shape[1]
    vmem = pl.BlockSpec(memory_space=pltpu.VMEM)
    hbm = pl.BlockSpec(memory_space=pltpu.HBM)
    dma = pltpu.SemaphoreType.DMA
    grad = jax.ShapeDtypeStruct((ROWS, width), F32)
    loss, image_grad, text_grad = pl.pallas_call(
        kernel,
        out_shape=(jax.ShapeDtypeStruct((8, 128), F32), grad, grad),
        in_specs=[hbm, hbm, hbm, hbm],
        out_specs=(vmem, vmem, vmem),
        scratch_shapes=[
            pltpu.VMEM((2 * SET, width), BF16),
            pltpu.VMEM((2, 4, 4, ROWS, width), BF16),
            pltpu.VMEM((SET, 2 * SET), BF16),
            pltpu.VMEM((SET, 2 * SET), F32),
            pltpu.VMEM((4, 4, ROWS, width), BF16),
            pltpu.VMEM((3, ROWS, CUT), F32),
            pltpu.VMEM((3, ROWS, width - CUT), F32),
            pltpu.VMEM((ROWS, width), F32),
            pltpu.VMEM((3, 3, ROWS, CUT), BF16),
            pltpu.VMEM((3, 3, ROWS, width - CUT), BF16),
            pltpu.VMEM((2, 3, ROWS, width), BF16),
            pltpu.VMEM((12 * ROWS, width), BF16),
            pltpu.VMEM((4 * ROWS, width), F32),
            pltpu.VMEM((3, 3 * ROWS, width), BF16),
            pltpu.VMEM((3 * ROWS, width), BF16),
            pltpu.VMEM((2, 3, ROWS, width), BF16),
            pltpu.VMEM((3, 8, 8, 128), F32),
            pltpu.VMEM((SENT, width), BF16),
            pltpu.SMEM((2, 1), F32),
            dma((4,)),
            dma,
            dma((GROUPS,)),
            pltpu.VMEM((4, 8, 128), F32),
            dma((4,)),
            dma((3,)),
            dma((3,)),
        ],
        compiler_params=pltpu.CompilerParams(
            collective_id=0, has_side_effects=True, vmem_limit_bytes=48 * 2**20
        ),
        name="pairs",
    )(
        pltpu.with_memory_space_constraint(image_embed, pltpu.HBM),
        pltpu.with_memory_space_constraint(text_embed, pltpu.HBM),
        logit_scale,
        logit_bias,
    )
    loss, image_grad, text_grad = pl.pallas_call(
        finish,
        out_shape=(jax.ShapeDtypeStruct((1, 128), F32), grad, grad),
        in_specs=[vmem, vmem, vmem],
        out_specs=(hbm, hbm, hbm),
        scratch_shapes=[dma((3,))],
        compiler_params=pltpu.CompilerParams(vmem_limit_bytes=2**20),
        name="finish",
    )(loss, image_grad, text_grad)
    return loss[0, 0:1], image_grad, text_grad


def solution(mesh):
    rows = P(("wide", "narrow"), None)
    return jax.shard_map(
        local, mesh=mesh, in_specs=(rows, rows, P(), P()), out_specs=(P(), rows, rows), check_vma=False
    )
```

```python
import jax
import jax.numpy as jnp
from jax import lax
from jax.experimental import pallas as pl
from jax.experimental.pallas import tpu as pltpu
from jax.sharding import PartitionSpec as P

MESH = pl.DeviceIdType.MESH
F32 = jnp.float32
BF16 = jnp.bfloat16
ROWS = 16
SET = 16 * ROWS
CUT = 640
SLOT = {1: 1, 3: 2, 2: 3}
GROUPS = 16
SENT = (30 + 30 + 32) * ROWS
NT = (((1,), (1,)), ((), ()))


def place():
    wide = lax.axis_index("wide")
    narrow = lax.axis_index("narrow")
    y = lax.rem(lax.div(wide, 2), 8)
    z = lax.div(wide, 16) * 4 + lax.rem(narrow, 4)
    return lax.div(narrow, 4), y, z, lax.rem(wide, 2)


def device(x, y, z, core):
    return (lax.div(z, 4) * 16 + y * 2 + core, x * 4 + lax.rem(z, 4))


def turned_logits(dots, scaling, offset, diagonal):
    logits = scaling * dots + offset
    return logits if diagonal is None else jnp.where(diagonal, -logits, logits)


def pair_weights(turned, scaling, diagonal):
    small = jnp.exp(-jnp.abs(turned))
    weights = scaling * (jnp.where(turned >= 0.0, 1.0, small) / (1.0 + small))
    if diagonal is not None:
        weights = jnp.where(diagonal, -weights, weights)
    return weights.astype(BF16)


def pair_loss(turned):
    terms = jnp.maximum(turned, 0.0) + jnp.log1p(jnp.exp(-jnp.abs(turned)))
    terms = jnp.sum(terms.reshape(-1, 8, terms.shape[-1]), axis=0)
    return sum(terms[:, k : k + 128] for k in range(0, terms.shape[-1], 128))


def kernel(
    image_ref,
    text_ref,
    scale_ref,
    bias_ref,
    loss_ref,
    image_grad_ref,
    text_grad_ref,
    images,
    texts,
    weights,
    kept,
    text_parts,
    text_near,
    text_far,
    text_own,
    came_z,
    came_y,
    last_text,
    image_parts,
    image_own,
    came_x,
    block_parts,
    last_image,
    totals,
    all_sent,
    numbers,
    load,
    send,
    recv,
    shared_loss,
    hop,
    loss_send,
    loss_recv,
):
    x, y, z, core = place()
    steps = (2, 1, 3)
    flipped_y = y + 1 - 2 * lax.rem(y, 2)
    flipped_z = z + 1 - 2 * lax.rem(z, 2)

    def along_x(k):
        return device(lax.rem(x + k, 4), y, z, core)

    def ring_y(k):
        return device(x, lax.rem(y + k, 8), z, core)

    def ring_z(k):
        return device(x, y, lax.rem(z + k, 8), core)

    def along_y(k):
        return ring_y(2 * k)

    def along_z(k):
        return ring_z(2 * k)

    def in_block(k):
        return device(x, flipped_y if k % 2 else y, flipped_z if k // 2 else z, core)

    sibling = device(x, y, z, 1 - core)

    barrier = pltpu.get_barrier_semaphore()
    for reach in (along_y, along_z, along_x, in_block):
        for k in steps:
            pl.semaphore_signal(barrier, inc=1, device_id=reach(k), device_id_type=MESH)
    pl.semaphore_signal(barrier, inc=1, device_id=sibling, device_id_type=MESH)
    loads = [
        pltpu.make_async_copy(image_ref, images.at[pl.ds(0, ROWS)], load.at[0]),
        pltpu.make_async_copy(text_ref, texts.at[0, 0, 0], load.at[1]),
        pltpu.make_async_copy(scale_ref, numbers.at[0], load.at[2]),
        pltpu.make_async_copy(bias_ref, numbers.at[1], load.at[3]),
    ]
    for made in loads:
        made.start()
    pl.semaphore_wait(barrier, 13)

    groups = []

    def start(whole, copies, group=None):
        if group is None:
            group = len(groups)
            groups.append(whole)
        for src, dst, to in copies:
            pltpu.make_async_remote_copy(
                src_ref=src,
                dst_ref=dst,
                send_sem=send,
                recv_sem=recv.at[group],
                device_id=to,
                device_id_type=MESH,
            ).start()
        return group

    def arrived(*which):
        for group in which:
            pltpu.make_async_copy(groups[group], groups[group], recv.at[group]).wait()

    width = texts.shape[-1]
    first, near, far, rest = pl.ds(0, 1), pl.ds(1, 2), pl.ds(3, 1), pl.ds(1, 3)
    head, tail = pl.ds(0, CUT), pl.ds(CUT, width - CUT)
    bundle = 4 * ROWS

    def own_text(part, reach, along_near, ways, group=None):
        def there(slots):
            return texts.at[0, first, slots, :, part] if along_near else texts.at[0, slots, first, :, part]

        def slot(k):
            at = SLOT[4 - k]
            return texts.at[0, 0, at, :, part] if along_near else texts.at[0, at, 0, :, part]

        return start(
            there(far if ways == (2,) else near), [(text_ref.at[:, part], slot(k), reach(k)) for k in ways], group
        )

    from_block = start(
        images.at[pl.ds(ROWS, 3 * ROWS)],
        [(image_ref, images.at[pl.ds(k * ROWS, ROWS)], in_block(k)) for k in (3, 1, 2)],
    )
    head_y_far = own_text(head, along_y, True, (2,))
    tail_z_far = own_text(tail, along_z, False, (2,))
    head_y = own_text(head, along_y, True, (1, 3))
    tail_z = own_text(tail, along_z, False, (1, 3))
    from_x = start(
        images.at[pl.ds(bundle, 3 * bundle)],
        [(image_ref, images.at[pl.ds((4 - k) * bundle, ROWS)], along_x(k)) for k in steps],
    )
    passed = start(texts.at[0, rest], [])
    own_text(tail, along_y, True, steps, passed)
    own_text(head, along_z, False, steps, passed)

    def pass_z(slots):
        start(
            texts.at[0, rest],
            [(texts.at[0, 0, slots, :, head], texts.at[0, SLOT[4 - k], slots, :, head], along_z(k)) for k in steps],
            passed,
        )

    def pass_y(slots):
        start(
            texts.at[0, rest],
            [(texts.at[0, slots, 0, :, tail], texts.at[0, slots, SLOT[4 - k], :, tail], along_y(k)) for k in steps],
            passed,
        )

    arrived(from_block)
    block = pl.ds(ROWS, 3 * ROWS)
    start(
        images.at[block],
        [
            (images.at[block], images.at[pl.ds((4 - k) * bundle + ROWS, 3 * ROWS)], along_x(k))
            for k in steps
        ],
        from_x,
    )
    arrived(head_y)
    pass_z(near)
    arrived(tail_z)
    pass_y(near)
    arrived(head_y_far)
    pass_z(far)
    arrived(tail_z_far)
    pass_y(far)
    for made in loads:
        made.wait()
    scaling = numbers[0, 0]
    offset = numbers[1, 0]
    arrived(from_x)
    image_share = start(
        images.at[pl.ds(SET, SET)], [(images.at[pl.ds(0, SET)], images.at[pl.ds(SET, SET)], sibling)]
    )
    arrived(passed)
    text_share = start(texts.at[1], [(texts.at[0], texts.at[1], sibling)])

    rows = lax.broadcasted_iota(jnp.int32, (SET, SET), 0)
    columns = lax.broadcasted_iota(jnp.int32, (SET, SET), 1)
    diagonal = (rows == columns) & (rows < ROWS)

    def in_plane(k):
        return device(lax.rem(x + k % 4, 4), lax.rem(y + 2 * (k // 4), 8), z, core)

    def in_column(k):
        return device(x, flipped_y if k % 2 else y, lax.rem(z + k // 2, 8), core)

    def plane_hops(k):
        return (0, 1, 2, 1)[k % 4] + (0, 2, 4, 2)[k // 4]

    def column_hops(k):
        return k % 2 + min(k // 2, 8 - k // 2)

    stages = (
        (4 * x + lax.div(y, 2), in_plane, sorted(range(1, 16), key=plane_hops, reverse=True)),
        (2 * z + lax.rem(y, 2), in_column, sorted(range(1, 16), key=column_hops, reverse=True)),
    )

    def across(src, dst, at):
        return pltpu.make_async_remote_copy(
            src_ref=src, dst_ref=dst, send_sem=hop.at[at], recv_sem=hop.at[at + 1], device_id=sibling, device_id_type=MESH
        )

    def ring(stage):
        slot, reach, ways = stages[stage]
        mine = totals.at[stage, slot]
        return [
            pltpu.make_async_remote_copy(
                src_ref=mine,
                dst_ref=mine,
                send_sem=loss_send.at[stage],
                recv_sem=loss_recv.at[stage],
                device_id=reach(k),
                device_id_type=MESH,
            )
            for k in ways
        ], totals.at[stage, pl.ds(0, len(ways))]

    def give(stage, value):
        totals[stage, stages[stage][0]] = value
        for made in ring(stage)[0]:
            made.start()

    def take(stage):
        whole = ring(stage)[1]
        pltpu.make_async_copy(whole, whole, loss_recv.at[stage]).wait()
        value = totals[stage, 0]
        for k in range(1, len(stages[stage][2]) + 1):
            value = value + totals[stage, k]
        return value

    def on_core_1(action):
        pl.when(core == 1)(action)

    def on_core_0(action):
        pl.when(core == 0)(action)

    def loss_start(value):
        shared_loss[0] = value
        on_core_0(across(shared_loss.at[0], shared_loss.at[1], 0).start)

    def loss_y():
        across(shared_loss.at[0], shared_loss.at[1], 0).wait_recv()
        give(0, shared_loss[0] + shared_loss[1])

    def loss_end():
        shared_loss[2] = take(1)
        across(shared_loss.at[2], shared_loss.at[3], 2).start()
        loss_ref[...] = jnp.full(loss_ref.shape, jnp.sum(shared_loss[2]) / 8192.0, F32)

    def loss_sent():
        across(shared_loss.at[2], shared_loss.at[3], 2).wait_send()
        for stage in range(2):
            whole = ring(stage)[1]
            pltpu.make_async_copy(whole, whole, loss_send.at[stage]).wait()

    def loss_got():
        across(shared_loss.at[2], shared_loss.at[3], 2).wait_recv()
        loss_ref[...] = jnp.full(loss_ref.shape, jnp.sum(shared_loss[3]) / 8192.0, F32)
        across(shared_loss.at[0], shared_loss.at[1], 0).wait_send()

    def text_set(half):
        return texts[half].reshape(SET, width)

    arrived(image_share)
    for half in (0, 1):
        part = slice(half * SET, (half + 1) * SET)
        mask = diagonal if half == 0 else None
        dots = lax.dot_general(text_set(0), images[part], NT, preferred_element_type=F32)
        turned = turned_logits(dots, scaling, offset, mask)
        kept[:, part] = turned
        weights[:, part] = pair_weights(turned, scaling, mask)
    loss_start(pair_loss(kept[...]))
    grads = jnp.dot(weights[...], images[...], preferred_element_type=F32).reshape(4, 4, ROWS, -1)
    text_parts[...] = grads.astype(BF16)
    text_near[...] = grads[0, 1:4, :, 0:CUT]
    text_far[...] = grads[1:4, 0, :, CUT:]
    text_own[...] = grads[0, 0]

    def to_z(there, here):
        return start(
            came_z.at[:, there],
            [(text_parts.at[SLOT[k], here, :, head], came_z.at[SLOT[4 - k] - 1, there], along_z(k)) for k in steps],
        )

    def to_y(there, here):
        return start(
            came_y.at[:, there],
            [(text_parts.at[here, SLOT[k], :, tail], came_y.at[SLOT[4 - k] - 1, there], along_y(k)) for k in steps],
        )

    to_z_far, to_y_far = to_z(pl.ds(2, 1), far), to_y(pl.ds(2, 1), far)
    to_z_near, to_y_near = to_z(pl.ds(0, 2), near), to_y(pl.ds(0, 2), near)

    on_core_1(loss_y)

    arrived(text_share)
    for half in (0, 1):
        dots = lax.dot_general(images[0:SET], text_set(half), NT, preferred_element_type=F32)
        mask = diagonal if half == 0 else None
        turned = turned_logits(dots, scaling, offset, mask)
        weights[:, half * SET : (half + 1) * SET] = pair_weights(turned, scaling, mask)
    grads = jnp.dot(weights[...], texts[...].reshape(2 * SET, width), preferred_element_type=F32)
    image_own[...] = grads[0:bundle]
    image_parts[...] = grads[bundle:].astype(BF16)
    to_x = start(
        came_x,
        [
            (image_parts.at[pl.ds((k - 1) * bundle + ROWS, 3 * ROWS)], came_x.at[3 - k], along_x(k))
            for k in steps
        ],
    )
    def out_y(slots, ways):
        for at in slots:
            total = text_near[at - 1]
            for k in range(3):
                total = total + came_z[k, at - 1].astype(F32)
            text_parts[0, at, :, 0:CUT] = total.astype(BF16)
        start(
            last_text,
            [(text_parts.at[0, SLOT[k], :, head], last_text.at[0, SLOT[4 - k] - 1, :, head], along_y(k)) for k in ways],
            text_end,
        )

    def out_z(slots, ways):
        for at in slots:
            total = text_far[at - 1]
            for k in range(3):
                total = total + came_y[k, at - 1].astype(F32)
            text_parts[at, 0, :, CUT:] = total.astype(BF16)
        start(
            last_text,
            [(text_parts.at[SLOT[k], 0, :, tail], last_text.at[1, SLOT[4 - k] - 1, :, tail], along_z(k)) for k in ways],
            text_end,
        )

    text_end = start(last_text, [])
    image_end = start(last_image, [])
    arrived(to_z_far)
    out_y((3,), (2,))
    arrived(to_y_far)
    out_z((3,), (2,))
    start(
        last_image,
        [(image_parts.at[pl.ds((k - 1) * bundle, ROWS)], last_image.at[0, 3 - k], along_x(k)) for k in steps],
        image_end,
    )
    start(
        last_text,
        [(text_parts.at[0, SLOT[k], :, tail], last_text.at[0, SLOT[4 - k] - 1, :, tail], along_y(k)) for k in steps]
        + [(text_parts.at[SLOT[k], 0, :, head], last_text.at[1, SLOT[4 - k] - 1, :, head], along_z(k)) for k in steps],
        text_end,
    )
    arrived(to_z_near)
    out_y((1, 2), (1, 3))
    arrived(to_y_near)
    out_z((1, 2), (1, 3))
    on_core_1(lambda: give(1, take(0)))
    arrived(to_x)
    total = image_own[ROWS:]
    for k in range(3):
        total = total + came_x[k].astype(F32)
    block_parts[...] = total.astype(BF16)
    start(
        last_image,
        [
            (block_parts.at[pl.ds((k - 1) * ROWS, ROWS)], last_image.at[1, k - 1], in_block(k))
            for k in (3, 1, 2)
        ],
        image_end,
    )
    arrived(text_end)
    total = text_own[...]
    for k in range(3):
        total = total + last_text[0, k].astype(F32) + last_text[1, k].astype(F32)
    text_grad_ref[...] = total
    on_core_1(loss_end)
    arrived(image_end)
    total = image_own[0:ROWS]
    for k in range(3):
        total = total + last_image[0, k].astype(F32) + last_image[1, k].astype(F32)
    image_grad_ref[...] = total
    on_core_1(loss_sent)
    on_core_0(loss_got)
    pltpu.make_async_copy(all_sent, all_sent, send).wait()


def finish(loss_ref, image_ref, text_ref, loss_out, image_out, text_out, sems):
    copies = [
        pltpu.make_async_copy(image_ref, image_out, sems.at[0]),
        pltpu.make_async_copy(text_ref, text_out, sems.at[1]),
        pltpu.make_async_copy(loss_ref.at[pl.ds(0, 1)], loss_out, sems.at[2]),
    ]
    for made in copies:
        made.start()
    for made in copies:
        made.wait()


def local(image_embed, text_embed, logit_scale, logit_bias):
    width = image_embed.shape[1]
    vmem = pl.BlockSpec(memory_space=pltpu.VMEM)
    hbm = pl.BlockSpec(memory_space=pltpu.HBM)
    dma = pltpu.SemaphoreType.DMA
    grad = jax.ShapeDtypeStruct((ROWS, width), F32)
    loss, image_grad, text_grad = pl.pallas_call(
        kernel,
        out_shape=(jax.ShapeDtypeStruct((8, 128), F32), grad, grad),
        in_specs=[hbm, hbm, hbm, hbm],
        out_specs=(vmem, vmem, vmem),
        scratch_shapes=[
            pltpu.VMEM((2 * SET, width), BF16),
            pltpu.VMEM((2, 4, 4, ROWS, width), BF16),
            pltpu.VMEM((SET, 2 * SET), BF16),
            pltpu.VMEM((SET, 2 * SET), F32),
            pltpu.VMEM((4, 4, ROWS, width), BF16),
            pltpu.VMEM((3, ROWS, CUT), F32),
            pltpu.VMEM((3, ROWS, width - CUT), F32),
            pltpu.VMEM((ROWS, width), F32),
            pltpu.VMEM((3, 3, ROWS, CUT), BF16),
            pltpu.VMEM((3, 3, ROWS, width - CUT), BF16),
            pltpu.VMEM((2, 3, ROWS, width), BF16),
            pltpu.VMEM((12 * ROWS, width), BF16),
            pltpu.VMEM((4 * ROWS, width), F32),
            pltpu.VMEM((3, 3 * ROWS, width), BF16),
            pltpu.VMEM((3 * ROWS, width), BF16),
            pltpu.VMEM((2, 3, ROWS, width), BF16),
            pltpu.VMEM((2, 16, 8, 128), F32),
            pltpu.VMEM((SENT, width), BF16),
            pltpu.SMEM((2, 1), F32),
            dma((4,)),
            dma,
            dma((GROUPS,)),
            pltpu.VMEM((4, 8, 128), F32),
            dma((4,)),
            dma((2,)),
            dma((2,)),
        ],
        compiler_params=pltpu.CompilerParams(
            collective_id=0, has_side_effects=True, vmem_limit_bytes=48 * 2**20
        ),
        name="pairs",
    )(
        pltpu.with_memory_space_constraint(image_embed, pltpu.HBM),
        pltpu.with_memory_space_constraint(text_embed, pltpu.HBM),
        logit_scale,
        logit_bias,
    )
    loss, image_grad, text_grad = pl.pallas_call(
        finish,
        out_shape=(jax.ShapeDtypeStruct((1, 128), F32), grad, grad),
        in_specs=[vmem, vmem, vmem],
        out_specs=(hbm, hbm, hbm),
        scratch_shapes=[dma((3,))],
        compiler_params=pltpu.CompilerParams(vmem_limit_bytes=2**20),
        name="finish",
    )(loss, image_grad, text_grad)
    return loss[0, 0:1], image_grad, text_grad


def solution(mesh):
    rows = P(("wide", "narrow"), None)
    return jax.shard_map(
        local, mesh=mesh, in_specs=(rows, rows, P(), P()), out_specs=(P(), rows, rows), check_vma=False
    )
```

```python
import jax
import jax.numpy as jnp
from jax import lax
from jax.experimental import pallas as pl
from jax.experimental.pallas import tpu as pltpu
from jax.sharding import PartitionSpec as P

MESH = pl.DeviceIdType.MESH
F32 = jnp.float32
BF16 = jnp.bfloat16
ROWS = 16
SET = 16 * ROWS
CUT = 640
SLOT = {1: 1, 3: 2, 2: 3}
GROUPS = 16
SENT = (30 + 30 + 32) * ROWS
NT = (((1,), (1,)), ((), ()))


def place():
    wide = lax.axis_index("wide")
    narrow = lax.axis_index("narrow")
    y = lax.rem(lax.div(wide, 2), 8)
    z = lax.div(wide, 16) * 4 + lax.rem(narrow, 4)
    return lax.div(narrow, 4), y, z, lax.rem(wide, 2)


def device(x, y, z, core):
    return (lax.div(z, 4) * 16 + y * 2 + core, x * 4 + lax.rem(z, 4))


def turned_logits(dots, scaling, offset, diagonal):
    logits = scaling * dots + offset
    return logits if diagonal is None else jnp.where(diagonal, -logits, logits)


def pair_weights(turned, scaling, diagonal):
    small = jnp.exp(-jnp.abs(turned))
    weights = scaling * (jnp.where(turned >= 0.0, 1.0, small) / (1.0 + small))
    if diagonal is not None:
        weights = jnp.where(diagonal, -weights, weights)
    return weights.astype(BF16)


def pair_loss(turned):
    terms = jnp.maximum(turned, 0.0) + jnp.log1p(jnp.exp(-jnp.abs(turned)))
    terms = jnp.sum(terms.reshape(-1, 8, terms.shape[-1]), axis=0)
    return sum(terms[:, k : k + 128] for k in range(0, terms.shape[-1], 128))


def kernel(
    image_ref,
    text_ref,
    scale_ref,
    bias_ref,
    loss_ref,
    image_grad_ref,
    text_grad_ref,
    images,
    texts,
    weights,
    kept,
    text_parts,
    text_near,
    text_far,
    text_own,
    came_z,
    came_y,
    last_text,
    image_parts,
    image_own,
    came_x,
    block_parts,
    last_image,
    totals,
    all_sent,
    numbers,
    load,
    send,
    recv,
    shared_loss,
    hop,
    loss_send,
    loss_recv,
):
    x, y, z, core = place()
    steps = (2, 1, 3)
    flipped_y = y + 1 - 2 * lax.rem(y, 2)
    flipped_z = z + 1 - 2 * lax.rem(z, 2)

    def along_x(k):
        return device(lax.rem(x + k, 4), y, z, core)

    def ring_y(k):
        return device(x, lax.rem(y + k, 8), z, core)

    def ring_z(k):
        return device(x, y, lax.rem(z + k, 8), core)

    def along_y(k):
        return ring_y(2 * k)

    def along_z(k):
        return ring_z(2 * k)

    def in_block(k):
        return device(x, flipped_y if k % 2 else y, flipped_z if k // 2 else z, core)

    sibling = device(x, y, z, 1 - core)

    barrier = pltpu.get_barrier_semaphore()
    for reach in (along_y, along_z, along_x, in_block):
        for k in steps:
            pl.semaphore_signal(barrier, inc=1, device_id=reach(k), device_id_type=MESH)
    pl.semaphore_signal(barrier, inc=1, device_id=sibling, device_id_type=MESH)
    loads = [
        pltpu.make_async_copy(image_ref, images.at[pl.ds(0, ROWS)], load.at[0]),
        pltpu.make_async_copy(text_ref, texts.at[0, 0, 0], load.at[1]),
        pltpu.make_async_copy(scale_ref, numbers.at[0], load.at[2]),
        pltpu.make_async_copy(bias_ref, numbers.at[1], load.at[3]),
    ]
    for made in loads:
        made.start()
    pl.semaphore_wait(barrier, 13)

    groups = []

    def start(whole, copies, group=None):
        if group is None:
            group = len(groups)
            groups.append(whole)
        for src, dst, to in copies:
            pltpu.make_async_remote_copy(
                src_ref=src,
                dst_ref=dst,
                send_sem=send,
                recv_sem=recv.at[group],
                device_id=to,
                device_id_type=MESH,
            ).start()
        return group

    def arrived(*which):
        for group in which:
            pltpu.make_async_copy(groups[group], groups[group], recv.at[group]).wait()

    width = texts.shape[-1]
    first, near, far, rest = pl.ds(0, 1), pl.ds(1, 2), pl.ds(3, 1), pl.ds(1, 3)
    head, tail = pl.ds(0, CUT), pl.ds(CUT, width - CUT)
    bundle = 4 * ROWS

    def own_text(part, reach, along_near, ways, group=None):
        def there(slots):
            return texts.at[0, first, slots, :, part] if along_near else texts.at[0, slots, first, :, part]

        def slot(k):
            at = SLOT[4 - k]
            return texts.at[0, 0, at, :, part] if along_near else texts.at[0, at, 0, :, part]

        return start(
            there(far if ways == (2,) else near), [(text_ref.at[:, part], slot(k), reach(k)) for k in ways], group
        )

    from_block = start(
        images.at[pl.ds(ROWS, 3 * ROWS)],
        [(image_ref, images.at[pl.ds(k * ROWS, ROWS)], in_block(k)) for k in (3, 1, 2)],
    )
    head_y_far = own_text(head, along_y, True, (2,))
    tail_z_far = own_text(tail, along_z, False, (2,))
    head_y = own_text(head, along_y, True, (1, 3))
    tail_z = own_text(tail, along_z, False, (1, 3))
    from_x = start(
        images.at[pl.ds(bundle, 3 * bundle)],
        [(image_ref, images.at[pl.ds((4 - k) * bundle, ROWS)], along_x(k)) for k in steps],
    )
    passed = start(texts.at[0, rest], [])
    own_text(tail, along_y, True, steps, passed)
    own_text(head, along_z, False, steps, passed)

    def pass_z(slots):
        start(
            texts.at[0, rest],
            [(texts.at[0, 0, slots, :, head], texts.at[0, SLOT[4 - k], slots, :, head], along_z(k)) for k in steps],
            passed,
        )

    def pass_y(slots):
        start(
            texts.at[0, rest],
            [(texts.at[0, slots, 0, :, tail], texts.at[0, slots, SLOT[4 - k], :, tail], along_y(k)) for k in steps],
            passed,
        )

    arrived(from_block)
    block = pl.ds(ROWS, 3 * ROWS)
    start(
        images.at[block],
        [
            (images.at[block], images.at[pl.ds((4 - k) * bundle + ROWS, 3 * ROWS)], along_x(k))
            for k in steps
        ],
        from_x,
    )
    arrived(head_y)
    pass_z(near)
    arrived(tail_z)
    pass_y(near)
    arrived(head_y_far)
    pass_z(far)
    arrived(tail_z_far)
    pass_y(far)
    for made in loads:
        made.wait()
    scaling = numbers[0, 0]
    offset = numbers[1, 0]
    arrived(from_x)
    image_share = start(
        images.at[pl.ds(SET, SET)], [(images.at[pl.ds(0, SET)], images.at[pl.ds(SET, SET)], sibling)]
    )
    arrived(passed)
    text_share = start(texts.at[1], [(texts.at[0], texts.at[1], sibling)])

    rows = lax.broadcasted_iota(jnp.int32, (SET, SET), 0)
    columns = lax.broadcasted_iota(jnp.int32, (SET, SET), 1)
    diagonal = (rows == columns) & (rows < ROWS)

    def in_plane(k):
        return device(lax.rem(x + k % 4, 4), lax.rem(y + 2 * (k // 4), 8), z, core)

    def in_column(k):
        return device(x, flipped_y if k % 2 else y, lax.rem(z + k // 2, 8), core)

    def plane_hops(k):
        return (0, 1, 2, 1)[k % 4] + (0, 2, 4, 2)[k // 4]

    def column_hops(k):
        return k % 2 + min(k // 2, 8 - k // 2)

    stages = (
        (4 * x + lax.div(y, 2), in_plane, sorted(range(1, 16), key=plane_hops, reverse=True)),
        (2 * z + lax.rem(y, 2), in_column, sorted(range(1, 16), key=column_hops, reverse=True)),
    )

    def across(src, dst, at):
        return pltpu.make_async_remote_copy(
            src_ref=src, dst_ref=dst, send_sem=hop.at[at], recv_sem=hop.at[at + 1], device_id=sibling, device_id_type=MESH
        )

    def ring(stage):
        slot, reach, ways = stages[stage]
        mine = totals.at[stage, slot]
        return [
            pltpu.make_async_remote_copy(
                src_ref=mine,
                dst_ref=mine,
                send_sem=loss_send.at[stage],
                recv_sem=loss_recv.at[stage],
                device_id=reach(k),
                device_id_type=MESH,
            )
            for k in ways
        ], totals.at[stage, pl.ds(0, len(ways))]

    def give(stage, value):
        totals[stage, stages[stage][0]] = value
        for made in ring(stage)[0]:
            made.start()

    def take(stage):
        whole = ring(stage)[1]
        pltpu.make_async_copy(whole, whole, loss_recv.at[stage]).wait()
        value = totals[stage, 0]
        for k in range(1, len(stages[stage][2]) + 1):
            value = value + totals[stage, k]
        return value

    def on_core_1(action):
        pl.when(core == 1)(action)

    def on_core_0(action):
        pl.when(core == 0)(action)

    def loss_start(value):
        shared_loss[0] = value
        on_core_0(across(shared_loss.at[0], shared_loss.at[1], 0).start)

    def loss_y():
        across(shared_loss.at[0], shared_loss.at[1], 0).wait_recv()
        give(0, shared_loss[0] + shared_loss[1])

    def loss_end():
        shared_loss[2] = take(1)
        across(shared_loss.at[2], shared_loss.at[3], 2).start()
        loss_ref[...] = jnp.full(loss_ref.shape, jnp.sum(shared_loss[2]) / 8192.0, F32)

    def loss_sent():
        across(shared_loss.at[2], shared_loss.at[3], 2).wait_send()
        for stage in range(2):
            whole = ring(stage)[1]
            pltpu.make_async_copy(whole, whole, loss_send.at[stage]).wait()

    def loss_got():
        across(shared_loss.at[2], shared_loss.at[3], 2).wait_recv()
        loss_ref[...] = jnp.full(loss_ref.shape, jnp.sum(shared_loss[3]) / 8192.0, F32)
        across(shared_loss.at[0], shared_loss.at[1], 0).wait_send()

    def text_set(half):
        return texts[half].reshape(SET, width)

    arrived(image_share)
    for half in (0, 1):
        part = slice(half * SET, (half + 1) * SET)
        mask = diagonal if half == 0 else None
        dots = lax.dot_general(text_set(0), images[part], NT, preferred_element_type=F32)
        turned = turned_logits(dots, scaling, offset, mask)
        kept[:, part] = turned
        weights[:, part] = pair_weights(turned, scaling, mask)
    loss_start(pair_loss(kept[...]))
    grads = jnp.dot(weights[...], images[...], preferred_element_type=F32).reshape(4, 4, ROWS, -1)
    text_parts[...] = grads.astype(BF16)
    text_near[...] = grads[0, 1:4, :, 0:CUT]
    text_far[...] = grads[1:4, 0, :, CUT:]
    text_own[...] = grads[0, 0]

    def to_z(there, here):
        return start(
            came_z.at[:, there],
            [(text_parts.at[SLOT[k], here, :, head], came_z.at[SLOT[4 - k] - 1, there], along_z(k)) for k in steps],
        )

    def to_y(there, here):
        return start(
            came_y.at[:, there],
            [(text_parts.at[here, SLOT[k], :, tail], came_y.at[SLOT[4 - k] - 1, there], along_y(k)) for k in steps],
        )

    to_z_far, to_y_far = to_z(pl.ds(2, 1), far), to_y(pl.ds(2, 1), far)
    to_z_near, to_y_near = to_z(pl.ds(0, 2), near), to_y(pl.ds(0, 2), near)

    on_core_1(loss_y)

    arrived(text_share)
    for half in (0, 1):
        dots = lax.dot_general(images[0:SET], text_set(half), NT, preferred_element_type=F32)
        mask = diagonal if half == 0 else None
        turned = turned_logits(dots, scaling, offset, mask)
        weights[:, half * SET : (half + 1) * SET] = pair_weights(turned, scaling, mask)
    grads = jnp.dot(weights[...], texts[...].reshape(2 * SET, width), preferred_element_type=F32)
    image_own[...] = grads[0:bundle]
    image_parts[...] = grads[bundle:].astype(BF16)
    to_x = start(
        came_x,
        [
            (image_parts.at[pl.ds((k - 1) * bundle + ROWS, 3 * ROWS)], came_x.at[3 - k], along_x(k))
            for k in steps
        ],
    )
    def out_y(slots, ways):
        for at in slots:
            total = text_near[at - 1]
            for k in range(3):
                total = total + came_z[k, at - 1].astype(F32)
            text_parts[0, at, :, 0:CUT] = total.astype(BF16)
        start(
            last_text,
            [(text_parts.at[0, SLOT[k], :, head], last_text.at[0, SLOT[4 - k] - 1, :, head], along_y(k)) for k in ways],
            text_end,
        )

    def out_z(slots, ways):
        for at in slots:
            total = text_far[at - 1]
            for k in range(3):
                total = total + came_y[k, at - 1].astype(F32)
            text_parts[at, 0, :, CUT:] = total.astype(BF16)
        start(
            last_text,
            [(text_parts.at[SLOT[k], 0, :, tail], last_text.at[1, SLOT[4 - k] - 1, :, tail], along_z(k)) for k in ways],
            text_end,
        )

    text_end = start(last_text, [])
    image_end = start(last_image, [])
    arrived(to_z_far)
    out_y((3,), (2,))
    arrived(to_y_far)
    out_z((3,), (2,))
    start(
        last_image,
        [(image_parts.at[pl.ds((k - 1) * bundle, ROWS)], last_image.at[0, 3 - k], along_x(k)) for k in steps],
        image_end,
    )
    start(
        last_text,
        [(text_parts.at[0, SLOT[k], :, tail], last_text.at[0, SLOT[4 - k] - 1, :, tail], along_y(k)) for k in steps]
        + [(text_parts.at[SLOT[k], 0, :, head], last_text.at[1, SLOT[4 - k] - 1, :, head], along_z(k)) for k in steps],
        text_end,
    )
    arrived(to_z_near)
    out_y((1, 2), (1, 3))
    on_core_1(lambda: give(1, take(0)))
    arrived(to_y_near)
    out_z((1, 2), (1, 3))
    arrived(to_x)
    total = image_own[ROWS:]
    for k in range(3):
        total = total + came_x[k].astype(F32)
    block_parts[...] = total.astype(BF16)
    start(
        last_image,
        [
            (block_parts.at[pl.ds((k - 1) * ROWS, ROWS)], last_image.at[1, k - 1], in_block(k))
            for k in (3, 1, 2)
        ],
        image_end,
    )
    on_core_1(loss_end)
    arrived(text_end)
    total = text_own[...]
    for k in range(3):
        total = total + last_text[0, k].astype(F32) + last_text[1, k].astype(F32)
    text_grad_ref[...] = total
    arrived(image_end)
    total = image_own[0:ROWS]
    for k in range(3):
        total = total + last_image[0, k].astype(F32) + last_image[1, k].astype(F32)
    image_grad_ref[...] = total
    on_core_1(loss_sent)
    on_core_0(loss_got)
    pltpu.make_async_copy(all_sent, all_sent, send).wait()


def finish(loss_ref, image_ref, text_ref, loss_out, image_out, text_out, sems):
    copies = [
        pltpu.make_async_copy(image_ref, image_out, sems.at[0]),
        pltpu.make_async_copy(text_ref, text_out, sems.at[1]),
        pltpu.make_async_copy(loss_ref.at[pl.ds(0, 1)], loss_out, sems.at[2]),
    ]
    for made in copies:
        made.start()
    for made in copies:
        made.wait()


def local(image_embed, text_embed, logit_scale, logit_bias):
    width = image_embed.shape[1]
    vmem = pl.BlockSpec(memory_space=pltpu.VMEM)
    hbm = pl.BlockSpec(memory_space=pltpu.HBM)
    dma = pltpu.SemaphoreType.DMA
    grad = jax.ShapeDtypeStruct((ROWS, width), F32)
    loss, image_grad, text_grad = pl.pallas_call(
        kernel,
        out_shape=(jax.ShapeDtypeStruct((8, 128), F32), grad, grad),
        in_specs=[hbm, hbm, hbm, hbm],
        out_specs=(vmem, vmem, vmem),
        scratch_shapes=[
            pltpu.VMEM((2 * SET, width), BF16),
            pltpu.VMEM((2, 4, 4, ROWS, width), BF16),
            pltpu.VMEM((SET, 2 * SET), BF16),
            pltpu.VMEM((SET, 2 * SET), F32),
            pltpu.VMEM((4, 4, ROWS, width), BF16),
            pltpu.VMEM((3, ROWS, CUT), F32),
            pltpu.VMEM((3, ROWS, width - CUT), F32),
            pltpu.VMEM((ROWS, width), F32),
            pltpu.VMEM((3, 3, ROWS, CUT), BF16),
            pltpu.VMEM((3, 3, ROWS, width - CUT), BF16),
            pltpu.VMEM((2, 3, ROWS, width), BF16),
            pltpu.VMEM((12 * ROWS, width), BF16),
            pltpu.VMEM((4 * ROWS, width), F32),
            pltpu.VMEM((3, 3 * ROWS, width), BF16),
            pltpu.VMEM((3 * ROWS, width), BF16),
            pltpu.VMEM((2, 3, ROWS, width), BF16),
            pltpu.VMEM((2, 16, 8, 128), F32),
            pltpu.VMEM((SENT, width), BF16),
            pltpu.SMEM((2, 1), F32),
            dma((4,)),
            dma,
            dma((GROUPS,)),
            pltpu.VMEM((4, 8, 128), F32),
            dma((4,)),
            dma((2,)),
            dma((2,)),
        ],
        compiler_params=pltpu.CompilerParams(
            collective_id=0, has_side_effects=True, vmem_limit_bytes=48 * 2**20
        ),
        name="pairs",
    )(
        pltpu.with_memory_space_constraint(image_embed, pltpu.HBM),
        pltpu.with_memory_space_constraint(text_embed, pltpu.HBM),
        logit_scale,
        logit_bias,
    )
    loss, image_grad, text_grad = pl.pallas_call(
        finish,
        out_shape=(jax.ShapeDtypeStruct((1, 128), F32), grad, grad),
        in_specs=[vmem, vmem, vmem],
        out_specs=(hbm, hbm, hbm),
        scratch_shapes=[dma((3,))],
        compiler_params=pltpu.CompilerParams(vmem_limit_bytes=2**20),
        name="finish",
    )(loss, image_grad, text_grad)
    return loss[0, 0:1], image_grad, text_grad


def solution(mesh):
    rows = P(("wide", "narrow"), None)
    return jax.shard_map(
        local, mesh=mesh, in_specs=(rows, rows, P(), P()), out_specs=(P(), rows, rows), check_vma=False
    )
```
